128 devices in a mesh: net: 4 (over x), line: 32 (over z, y, core).
Axes of the slice: x: 4, y: 4, z: 4, core: 2. Of those that a mesh axis runs over, the one named last changes fastest.
Arguments:
- conductance_inverse: float32 [4, 4096, 4096], P('net', 'line'), may hold values from -0.5 to 4.5, as said below
- prior_voltage: float32 [4, 96, 4096], P('net', None, 'line'), may hold values from -6 to 6
- sources: float32 [3, 4, 4096], P(None, 'net', 'line'), may hold values from -6 to 6
- fault_node: int32 [96], replicated, may hold values from 0 to 16383
- fault_conductance: float32 [96], replicated, may hold values from 0.5 to 4
- terminal_node: int32 [4, 3, 16384], P('net', None, 'line'), may hold values from 0 to 4095
- ownership: int32 [4, 16384], P('net', 'line'), may hold values from 0 to 1, as said below
- partner: int32 [4, 16384], P('net', 'line'), may hold values from 0 to 127, as said below
- delay_steps: int32 [4, 16384], P('net', 'line'), may hold values from 1 to 4, as said below
- surge_conductance: float32 [4, 16384], P('net', 'line'), may hold values from 0.2 to 1
- pole_wave: float32 [4, 6, 16384], P('net', None, 'line'), may hold values from 0.2 to 0.95
- residue_wave: float32 [4, 6, 3, 3, 16384], P('net', None, None, None, 'line'), may hold values from -1 to 1
- pole_admit: float32 [4, 6, 16384], P('net', None, 'line'), may hold values from 0.2 to 0.95
- residue_admit: float32 [4, 6, 3, 3, 16384], P('net', None, None, None, 'line'), may hold values from -1 to 1
- wave_state: float32 [4, 6, 3, 96, 16384], P('net', None, None, None, 'line'), may hold values from -4 to 4
- admit_state: float32 [4, 6, 3, 96, 16384], P('net', None, None, None, 'line'), may hold values from -4 to 4
- wave_history: float32 [4, 4, 3, 96, 16384], P('net', None, None, None, 'line'), may hold values from -6 to 6
Outputs:
- final_voltage: float32 [4, 96, 4096], P('net', None, 'line')
- end_current: float32 [4, 3, 96, 16384], P('net', None, None, 'line')
The draws below stay inside these ranges and needn't reach their ends.
Inputs may be any that keep to these rules, and one draw needn't show every extreme that they name: `conductance_inverse`: each block is exactly symmetric. `ownership`: A slot is live exactly when the slot of the same number j % 512 at its partner owner is live; the number of live slots differs from owner to owner. The far end of slot j lies in the slot of the same number j % 512 at the partner owner, the partner of that slot is the first owner again, never the owner itself, and at most 5 live slots of one owner have the same partner; this many occur. `delay_steps`: equal at both ends of a line.
All inputs are finite; a program needn't handle non-finite values.
Results may differ from the reference program's by a relative error of at most 0.0003.
Values sent between devices are 32-bit elements; how exact they have to be, the bound alone decides.
No kernel may reach another device: no remote copies, remote signals or barrier semaphores. Data moves between devices by JAX's collectives and lax.ppermute only.
A program may use at most 128 MiB of HBM per device.

```python
import math
from functools import partial
import jax
import jax.numpy as jnp
from jax import lax

NODES = 4096
SCENARIOS = 96
POLES = 6
STEPS = 3
DELAY_MAX = 4
SLOTS = 512
SUBS = 4
LINE_SLOTS = 16384
N_LINE = 32


def pair_tables(key):
    devices = SUBS * (LINE_SLOTS // SLOTS)
    anchor = jax.random.randint(jax.random.fold_in(key, 101), (), 0, devices)
    others = jax.random.permutation(jax.random.fold_in(key, 102), devices - 2) + 2
    flip_table = jnp.concatenate([jnp.ones((1,), jnp.int32), others.astype(jnp.int32)])
    slot_range = jnp.arange(SLOTS, dtype=jnp.int32)
    flip_mask = flip_table[slot_range % (devices - 1)]
    device_range = jnp.arange(devices, dtype=jnp.int32)
    partners = jnp.bitwise_xor(device_range[:, None], flip_mask[None, :])
    relabel = jnp.bitwise_xor(device_range, anchor)
    lowest = SLOTS // 6
    counts = jnp.where(relabel < 2, SLOTS, lowest + (relabel - 2) * (SLOTS - lowest) // (devices - 2))
    is_live = (slot_range[None, :] < counts[:, None]) & (slot_range[None, :] < counts[partners])
    return (partners, is_live, device_range, slot_range)


def draw_ownership(key, part):
    partners, is_live, device_range, slot_range = pair_tables(key)
    return is_live.astype(jnp.int32).reshape(SUBS, LINE_SLOTS)


def draw_partner(key, part):
    partners, is_live, device_range, slot_range = pair_tables(key)
    return partners.astype(jnp.int32).reshape(SUBS, LINE_SLOTS)


def draw_delay_steps(key, part):
    partners, is_live, device_range, slot_range = pair_tables(key)
    table = jax.random.randint(jax.random.fold_in(key, 103), partners.shape, 1, DELAY_MAX + 1)
    lower = jnp.minimum(device_range[:, None], partners)
    delays = table[lower, slot_range[None, :]]
    return delays.astype(jnp.int32).reshape(SUBS, LINE_SLOTS)


def draw_conductance_inverse(key, part):

    def one_block(index):
        block_key = jax.random.fold_in(key, index + 7)
        raw = jax.random.normal(jax.random.fold_in(block_key, 1), (NODES, NODES), jnp.float32)
        spread = (raw + raw.T) * (0.008 / math.sqrt(2.0))
        diagonal = jnp.exp(jax.random.uniform(jax.random.fold_in(block_key, 2), (NODES,), jnp.float32, math.log(1.5), math.log(4.0)))
        return spread + jnp.diag(diagonal)
    return lax.map(one_block, jnp.arange(SUBS, dtype=jnp.int32)).astype(jnp.float32)


def touch_ends(result, rng, smallest, high):
    longest = result.shape.index(max(result.shape))
    spots = []
    for shift in (0, 1):
        where = [jax.random.randint(jax.random.fold_in(rng, axis), (), 0, length) for axis, length in enumerate(result.shape)]
        where[longest] = (where[longest] + shift) % result.shape[longest]
        spots.append(tuple(where))
    return result.at[spots[0]].set(smallest).at[spots[1]].set(high)


def levels(own_key, extent, pieces, smallest, high):
    def one(axis_at, parts):
        draws = jax.random.uniform(jax.random.fold_in(jax.random.fold_in(own_key, 6), axis_at), (parts,), jnp.float32, smallest / len(pieces), high / len(pieces))
        return jnp.repeat(jnp.exp(draws), extent[axis_at] // parts).reshape((-1,) + (1,) * (len(extent) - axis_at - 1))

    loudness = one(*pieces[0])
    for cut in pieces[1:]:
        loudness = loudness * one(*cut)
    return loudness


def noise(own_key, dims, scale, bound, cuts=(), kind=jnp.bfloat16):
    loudness = levels(own_key, dims, cuts, -0.22, 0.18) if cuts else 1.0
    result = jax.random.normal(own_key, dims, jnp.float32) * scale * loudness
    return jnp.minimum(jnp.maximum(result, -bound), bound).astype(kind)


def setup_inputs(seed: int = 0) -> dict:
    splits = jax.random.split(jax.random.key(seed), 18)
    conductance_inverse = draw_conductance_inverse(jax.random.fold_in(splits[17], 71), 0)
    prior_voltage = noise(splits[1], (SUBS, SCENARIOS, NODES), 1.0, 6.0, ((0, 4), (2, 32)), jnp.float32)
    sources = noise(splits[2], (STEPS, SUBS, NODES), 1.0, 6.0, ((1, 4), (2, 32)), jnp.float32)
    fault_node = touch_ends(jax.random.randint(splits[3], (SCENARIOS,), 0, SUBS * NODES), jax.random.fold_in(splits[3], 1), 0, (SUBS * NODES) - 1).astype(jnp.int32)
    fault_conductance = jnp.clip(jnp.exp(jax.random.uniform(splits[4], (SCENARIOS,), jnp.float32, math.log(0.5), math.log(4.0))), 0.5, 4.0)
    terminal_node = touch_ends(jax.random.randint(splits[5], (SUBS, 3, LINE_SLOTS), 0, NODES), jax.random.fold_in(splits[5], 1), 0, NODES - 1).astype(jnp.int32)
    ownership = draw_ownership(jax.random.fold_in(splits[17], 71), 0)
    partner = draw_partner(jax.random.fold_in(splits[17], 71), 0)
    delay_steps = draw_delay_steps(jax.random.fold_in(splits[17], 71), 0)
    surge_conductance = jnp.clip(jnp.exp(math.log(1.0) - 1.609438 * jax.random.uniform(splits[9], (SUBS, LINE_SLOTS), jnp.float32) ** levels(splits[9], (SUBS, LINE_SLOTS), ((0, 4), (1, 32)), -0.2, 0.2)), 0.2, 1.0)
    pole_wave = jnp.clip(jnp.exp(math.log(0.95) - 1.5581446 * jax.random.uniform(splits[10], (SUBS, POLES, LINE_SLOTS), jnp.float32) ** levels(splits[10], (SUBS, POLES, LINE_SLOTS), ((0, 4), (2, 32)), -0.2, 0.2)), 0.2, 0.95)
    residue_wave = noise(splits[11], (SUBS, POLES, 3, 3, LINE_SLOTS), 0.15, 1.0, ((0, 4), (4, 32)), jnp.float32)
    pole_admit = jnp.clip(jnp.exp(math.log(0.95) - 1.5581446 * jax.random.uniform(splits[12], (SUBS, POLES, LINE_SLOTS), jnp.float32) ** levels(splits[12], (SUBS, POLES, LINE_SLOTS), ((0, 4), (2, 32)), -0.2, 0.2)), 0.2, 0.95)
    residue_admit = noise(splits[13], (SUBS, POLES, 3, 3, LINE_SLOTS), 0.15, 1.0, ((0, 4), (4, 32)), jnp.float32)
    wave_state = noise(splits[14], (SUBS, POLES, 3, SCENARIOS, LINE_SLOTS), 0.5, 4.0, ((0, 4), (4, 32)), jnp.float32)
    admit_state = noise(splits[15], (SUBS, POLES, 3, SCENARIOS, LINE_SLOTS), 0.5, 4.0, ((0, 4), (4, 32)), jnp.float32)
    wave_history = noise(splits[16], (SUBS, DELAY_MAX, 3, SCENARIOS, LINE_SLOTS), 1.0, 6.0, ((0, 4), (4, 32)), jnp.float32)
    return {"conductance_inverse": conductance_inverse, "prior_voltage": prior_voltage, "sources": sources, "fault_node": fault_node, "fault_conductance": fault_conductance, "terminal_node": terminal_node, "ownership": ownership, "partner": partner, "delay_steps": delay_steps, "surge_conductance": surge_conductance, "pole_wave": pole_wave, "residue_wave": residue_wave, "pole_admit": pole_admit, "residue_admit": residue_admit, "wave_state": wave_state, "admit_state": admit_state, "wave_history": wave_history}


def mix_residue(residue, vector):
    return (residue[:, :, 0, None, :] * vector[0] + residue[:, :, 1, None, :] * vector[1]
            + residue[:, :, 2, None, :] * vector[2])


def select_delayed(buffer, delay_local):
    depth_count = buffer.shape[0]
    chosen = delay_local[None, :] == jnp.arange(1, depth_count + 1, dtype=jnp.int32)[:, None]
    return jnp.sum(jnp.where(chosen[:, None, None, :], buffer, 0.0), axis=0)


def terminal_values(voltage, terminal):
    picked = jnp.take(voltage, terminal.reshape(-1), axis=1)
    return jnp.moveaxis(picked.reshape(voltage.shape[0], 3, -1), 0, 1)


def spread_ends(history, terminal, node_count):
    values = jnp.moveaxis(history, 0, 1).reshape(history.shape[1], -1)
    return jnp.zeros((history.shape[1], node_count), jnp.float32).at[:, terminal.reshape(-1)].add(values)


def split_devices(array):
    leading = array.shape[0]
    middle = array.shape[1:-1]
    shaped = array.reshape((leading,) + middle + (N_LINE, array.shape[-1] // N_LINE))
    shaped = jnp.moveaxis(shaped, -2, 1)
    return shaped.reshape((leading * N_LINE,) + middle + (shaped.shape[-1],))


def join_devices(array):
    leading = array.shape[0] // N_LINE
    middle = array.shape[1:-1]
    shaped = array.reshape((leading, N_LINE) + middle + (array.shape[-1],))
    shaped = jnp.moveaxis(shaped, 1, -2)
    return shaped.reshape((leading,) + middle + (N_LINE * array.shape[-1],))


def solve_block(operands):
    return lax.dot_general(operands[0], operands[1], (((1,), (1,)), ((), ())),
                           precision=lax.Precision.HIGHEST, preferred_element_type=jnp.float32)


def reference(conductance_inverse, prior_voltage, sources, fault_node, fault_conductance, terminal_node,
              ownership, partner, delay_steps, surge_conductance, pole_wave, residue_wave, pole_admit,
              residue_admit, wave_state, admit_state, wave_history):
    live_float = split_devices(ownership).astype(jnp.float32)
    terminal_dev = split_devices(terminal_node)
    partner_dev = split_devices(partner)
    delay_dev = split_devices(delay_steps)
    surge_dev = split_devices(surge_conductance)
    wave_decay = split_devices(pole_wave)[:, :, None, None, :]
    admit_decay = split_devices(pole_admit)[:, :, None, None, :]
    wave_res = split_devices(residue_wave)
    admit_res = split_devices(residue_admit)
    wave_now = split_devices(wave_state)
    admits = split_devices(admit_state)
    history_buffer = split_devices(wave_history)
    slot_count = live_float.shape[1]
    slot_range = jnp.arange(slot_count, dtype=jnp.int32)
    scenario_range = jnp.arange(prior_voltage.shape[1], dtype=jnp.int32)
    fault_sub = fault_node // NODES
    fault_local = fault_node % NODES
    voltage = prior_voltage
    outgoing = None
    current = None
    mixer = jax.vmap(mix_residue)
    for step_index in range(STEPS):
        if step_index > 0:
            by_slot = jnp.moveaxis(outgoing, 3, 1)
            far_waves = by_slot[partner_dev, slot_range[None, :]]
            arrived = jnp.moveaxis(far_waves, 1, 3) * live_float[:, None, None, :]
            history_buffer = jnp.concatenate([arrived[:, None], history_buffer[:, :-1]], axis=1)
        incoming = jax.vmap(select_delayed)(history_buffer, delay_dev)
        voltage_dev = jnp.repeat(voltage, N_LINE, axis=0)
        terminal_prior = jax.vmap(terminal_values)(voltage_dev, terminal_dev)
        wave_now = wave_decay * wave_now + mixer(wave_res, incoming)
        admits = admit_decay * admits + mixer(admit_res, terminal_prior)
        history = (jnp.sum(wave_now, axis=1) - jnp.sum(admits, axis=1)) * live_float[:, None, None, :]
        injection = jax.vmap(partial(spread_ends, node_count=NODES))(join_devices(history), terminal_node)
        injection = injection + sources[step_index][:, None, :]
        fault_value = voltage[fault_sub, scenario_range, fault_local]
        injection = injection.at[fault_sub, scenario_range, fault_local].add(-fault_conductance * fault_value)
        voltage = lax.map(solve_block, (injection, conductance_inverse))
        voltage_dev = jnp.repeat(voltage, N_LINE, axis=0)
        terminal_now = jax.vmap(terminal_values)(voltage_dev, terminal_dev)
        if step_index + 1 < STEPS:
            outgoing = (2.0 * surge_dev[:, None, None, :] * terminal_now - history) * live_float[:, None, None, :]
        else:
            current = (surge_dev[:, None, None, :] * terminal_now - history) * live_float[:, None, None, :]
    return voltage, join_devices(current)
```

```python
import functools

import jax
import jax.numpy as jnp
from jax import lax
from jax.experimental import pallas as pl
from jax.experimental.pallas import tpu as pltpu
from jax.sharding import Mesh
from jax.sharding import PartitionSpec as P

STEPS = 3
LINE = ("z", "y", "core")
NET_LINE = ("net", "z", "y", "core")
SIDE = 4
CAPACITY = 5
F32 = jnp.float32
BF16 = jnp.bfloat16
VMEM = pl.BlockSpec(memory_space=pltpu.VMEM)
SMEM = pl.BlockSpec(memory_space=pltpu.SMEM)
PARAMS = pltpu.CompilerParams(vmem_limit_bytes=32 * 1024 * 1024)


def shape(*dims, dtype=F32):
    return jax.ShapeDtypeStruct(dims, dtype)


def call(kernel, scalars, arrays, outs, scratch=()):
    return pl.pallas_call(
        kernel,
        out_shape=outs,
        in_specs=[SMEM] * len(scalars) + [VMEM] * len(arrays),
        out_specs=jax.tree.map(lambda _: VMEM, outs),
        scratch_shapes=list(scratch),
        compiler_params=PARAMS,
    )(*scalars, *arrays)


def halves(x):
    high = x.astype(BF16)
    low = (x - high.astype(F32)).astype(BF16)
    return high, low


def stacked(x):
    return jnp.concatenate(halves(x), axis=0)


def ones_where(mask):
    return jnp.where(mask, 1.0, 0.0).astype(BF16)


def dot(a, b, dims):
    return lax.dot_general(a, b, (dims, ((), ())), preferred_element_type=F32)


NN = ((1,), (0,))
NT = ((1,), (1,))
TN = ((0,), (0,))


def mix(coef, waves):
    return [
        coef[p, 0:1, :] * waves[0] + coef[p, 1:2, :] * waves[1] + coef[p, 2:3, :] * waves[2]
        for p in range(3)
    ]


def fold_kernel(own, delay, pw, rw, pa, ra, xw, xa, hist, h_out, ka_out, e_out):
    live = own[...]
    steps = delay[...]
    kw, ka = [], []
    for pole, res, into in ((pw, rw, kw), (pa, ra, ka)):
        for p in range(3):
            into.append([])
            power = None
            for m in range(STEPS):
                total = None
                for q in range(pole.shape[0]):
                    term = res[q, p]
                    for _ in range(m):
                        term = term * pole[q : q + 1, :]
                    total = term if total is None else total + term
                into[p].append(total * live)
    first = (steps == 1).astype(F32)
    second = (steps == 2).astype(F32)
    for p in range(3):
        for m in range(STEPS):
            ka_out[m, p] = ka[p][m]
        e_out[0, p] = kw[p][0] * first
        e_out[1, p] = kw[p][1] * first + kw[p][0] * second
    delayed = []
    for age in range(STEPS):
        rows = []
        for r in range(3):
            w = None
            for k in range(hist.shape[0] - age):
                part = jnp.where(steps == k + 1 + age, hist[k, r], 0.0)
                w = part if w is None else w + part
            rows.append(w)
        delayed.append(rows)
    for p in range(3):
        totals = [None] * STEPS
        for q in range(pw.shape[0]):
            w_pole = pw[q : q + 1, :]
            a_pole = pa[q : q + 1, :]
            w_now = xw[q, p]
            a_now = xa[q, p]
            for t in range(STEPS):
                w_now = w_now * w_pole
                a_now = a_now * a_pole
                part = w_now - a_now
                totals[t] = part if totals[t] is None else totals[t] + part
        for t in range(STEPS):
            value = totals[t] * live
            for s in range(t + 1):
                for r in range(3):
                    value = value + kw[p][t - s][r : r + 1, :] * delayed[s][r]
            h_out[t, p] = value


def fold(own, delay, pw, rw, pa, ra, xw, xa, hist):
    poles, _, scenarios, slots = xw.shape
    tile = 16
    whole = lambda *dims: pl.BlockSpec(dims, lambda i: (0,) * len(dims))
    state = pl.BlockSpec((poles, 3, tile, slots), lambda i: (0, 0, i, 0))
    return pl.pallas_call(
        fold_kernel,
        grid=(scenarios // tile,),
        out_shape=(
            shape(STEPS, 3, scenarios, slots),
            shape(STEPS, 3, 3, slots),
            shape(2, 3, 3, slots),
        ),
        in_specs=[
            whole(1, slots),
            whole(1, slots),
            whole(poles, slots),
            whole(poles, 3, 3, slots),
            whole(poles, slots),
            whole(poles, 3, 3, slots),
            state,
            state,
            pl.BlockSpec((hist.shape[0], 3, tile, slots), lambda i: (0, 0, i, 0)),
        ],
        out_specs=(
            pl.BlockSpec((STEPS, 3, tile, slots), lambda i: (0, 0, i, 0)),
            whole(STEPS, 3, 3, slots),
            whole(2, 3, 3, slots),
        ),
        compiler_params=PARAMS,
    )(own, delay, pw, rw, pa, ra, xw, xa, hist)


def inverse_kernel(ids, inverse, out):
    rows = inverse.shape[0]
    for k in range(inverse.shape[1] // 128):
        block = inverse[:, pl.ds(pl.multiple_of(ids[k] * 128, 128), 128)]
        high, low = halves(block)
        out[0:rows, k * 128 : (k + 1) * 128] = high
        out[rows : 2 * rows, k * 128 : (k + 1) * 128] = low


def gather_into(ids, terminal, volts, split, emit):
    count, scenarios, lanes = volts.shape
    for k in range(count):
        high, low = halves(volts[k])
        split[0:scenarios, k * lanes : (k + 1) * lanes] = high
        split[scenarios : 2 * scenarios, k * lanes : (k + 1) * lanes] = low
    width = 256
    local = lax.broadcasted_iota(jnp.int32, (lanes, width), 0)
    for p in range(3):
        for n in range(terminal.shape[1] // width):
            cut = slice(n * width, (n + 1) * width)
            nodes = terminal[p : p + 1, cut]
            hot = jnp.concatenate(
                [ones_where(local == nodes - ids[k] * lanes) for k in range(count)], axis=0
            )
            both = dot(split[...], hot, NN)
            emit(p, cut, both[:scenarios] + both[scenarios:])


def gather_kernel(ids, terminal, volts, out, split):
    def emit(p, cut, value):
        out[p, :, cut] = value

    gather_into(ids, terminal, volts, split, emit)


def gather_rest(ids, terminal, volts, before, out, split):
    def emit(p, cut, value):
        out[p, :, cut] = before[p, :, cut] + value

    gather_into(ids, terminal, volts, split, emit)


def scatter_into(ids, nodes, split, emit):
    ends = split.shape[1]
    scenarios = split.shape[0] // 2
    local = lax.broadcasted_iota(jnp.int32, (128, ends), 0)
    for k in range(0, 16, 2):
        hot = jnp.concatenate(
            [ones_where(local == nodes - ids[k + i] * 128) for i in range(2)], axis=0
        )
        both = dot(split, hot, NT)
        value = both[:scenarios] + both[scenarios:]
        for i in range(2):
            emit(k + i, value[:, i * 128 : (i + 1) * 128])


def split_ends(h):
    parts = [stacked(h[p]) for p in range(3)]
    return jnp.concatenate(parts, axis=1)


def scatter_other(ids, nodes, h, out, split):
    def emit(k, value):
        out[k] = value

    split[...] = split_ends(h)
    scatter_into(ids, nodes[...], split[...], emit)


def first_kernel(ids, to, terminal, nodes, volts, before, base, ka, term, h_out, out, split, ends):
    gather_rest(ids, terminal, volts, before, term, split)
    drop = mix(ka, term)
    for p in range(3):
        h_out[p] = base[p] - drop[p]
    scatter_other(to, nodes, h_out, out, ends)


def scatter_mine(ids, own, nodes, h, source, fault, conductance, volts, out, split):
    def emit(k, value):
        out[k] = value

    split[...] = split_ends(h)
    scatter_into(ids, nodes[...], split[...], emit)
    lane = lax.broadcasted_iota(jnp.int32, volts.shape, 1)
    drawn = jnp.where(lane == fault[...], conductance[...] * volts[...], 0.0)
    me = own[0]
    out[me] = out[me] + source[...] - drawn


def hot_places(places, count):
    owner = lax.broadcasted_iota(jnp.int32, (count, places.shape[1]), 0)
    return [ones_where(owner * 8 + r == places) for r in range(CAPACITY)]


def pack_kernel(ids, terminal, places, volts, before, surge2, h, term, packed, split):
    gather_rest(ids, terminal, volts, before, term, split)
    waves = [surge2[...] * term[p] - h[p] for p in range(3)]
    high, low = halves(jnp.concatenate(waves, axis=0))
    rows = []
    for hot in hot_places(places[...], packed.shape[0]):
        rows.append(dot(hot, high, NT) + dot(hot, low, NT))
    used = sum(r.shape[1] for r in rows)
    rows.append(jnp.zeros((packed.shape[0], packed.shape[1] - used), F32))
    packed[...] = jnp.concatenate(rows, axis=1)


def known_1(base, ka, t0, t1, out):
    a, b = mix(ka[1], t0), mix(ka[0], t1)
    for p in range(3):
        out[p] = base[p] - a[p] - b[p]


def known_2(base, ka, t0, t1, t2, e, a1, out):
    a, b, c, d = mix(ka[2], t0), mix(ka[1], t1), mix(ka[0], t2), mix(e[1], a1)
    for p in range(3):
        out[p] = base[p] - a[p] - b[p] - c[p] + d[p]


def arrive_kernel(to, nodes, places, packed, base, e, arrived, h_out, out, ends):
    scenarios = base.shape[1]
    wide = 3 * scenarios
    total = None
    for r, hot in enumerate(hot_places(places[...], packed.shape[0])):
        high, low = halves(packed[:, r * wide : (r + 1) * wide])
        part = dot(high, hot, TN) + dot(low, hot, TN)
        total = part if total is None else total + part
    for p in range(3):
        arrived[p] = total[p * scenarios : (p + 1) * scenarios]
    gain = mix(e[0], arrived)
    for p in range(3):
        h_out[p] = base[p] + gain[p]
    scatter_other(to, nodes, h_out, out, ends)


def last_kernel(ids, terminal, volts, before, surge, h, out, split):
    def emit(p, cut, value):
        term = before[p, :, cut] + value
        out[p, :, cut] = surge[:, cut] * term - h[p, :, cut]

    gather_into(ids, terminal, volts, split, emit)


def join_kernel(mine, other, *outs):
    for k, out in enumerate(outs):
        for z in range(SIDE):
            out[z] = mine[k * SIDE + z] + other[k * SIDE + z]


def solve_into(current, inverse, part, split):
    count, scenarios, lanes = current.shape
    for k in range(count):
        high, low = halves(current[k])
        split[0:scenarios, k * lanes : (k + 1) * lanes] = high
        split[scenarios : 2 * scenarios, k * lanes : (k + 1) * lanes] = low
    width = count * lanes
    both = dot(split[...], inverse[:, part * width : (part + 1) * width], NT)
    return both[:scenarios, :lanes] + both[:scenarios, lanes:] + both[scenarios:, :lanes]


def solve_first(current, inverse, out, split):
    out[...] = solve_into(current, inverse, 0, split)


def solve_rest(current, inverse, before, out, split):
    out[...] = before[...] + solve_into(current, inverse, 1, split)


def shifted(x, axis, shift):
    return lax.ppermute(x, axis, [(i, (i + shift) % SIDE) for i in range(SIDE)])


def swapped(x):
    return lax.ppermute(x, "core", [(0, 1), (1, 0)])


def around(x, axis):
    return [x] + [shifted(x, axis, k) for k in range(1, SIDE)]


def on_device(
    conductance_inverse,
    prior_voltage,
    sources,
    fault_node,
    fault_conductance,
    terminal_node,
    ownership,
    partner,
    delay_steps,
    surge_conductance,
    pole_wave,
    residue_wave,
    pole_admit,
    residue_admit,
    wave_state,
    admit_state,
    wave_history,
):
    rows, node_count = conductance_inverse.shape[1:]
    scenarios = prior_voltage.shape[1]
    slots = ownership.shape[1]
    ends = 3 * slots
    devices = lax.axis_size(NET_LINE)
    net, z, y, core = (lax.axis_index(a) for a in NET_LINE)
    me = lax.axis_index(LINE)

    live = ownership[0] > 0
    live_float = live.astype(F32)[None]
    partners = partner[0]
    slot = jnp.arange(slots, dtype=jnp.int32)
    earlier = (
        (partners[:, None] == partners[None, :])
        & live[:, None]
        & (slot[:, None] < slot[None, :])
    )
    rank = jnp.sum(earlier.astype(jnp.int32), axis=0)
    places = jnp.where(live, partners * 8 + rank, -1)[None]
    terminal = terminal_node[0]
    nodes = terminal.reshape(1, ends)
    surge = surge_conductance * live_float
    surge2 = 2.0 * surge
    fault = (fault_node - (net * node_count + me * rows))[:, None]
    conductance = fault_conductance[:, None]

    turn = jnp.arange(SIDE, dtype=jnp.int32)
    behind_z, behind_y = (z - turn) % SIDE, (y - turn) % SIDE

    def blocks(ys, zs, c):
        return ((zs[None, :] * SIDE + ys[:, None]) * 2 + c).reshape(-1)

    to_mine = blocks((y + turn) % SIDE, turn, core)
    to_other = blocks((y + turn) % SIDE, turn, 1 - core)
    from_mine = blocks(behind_y, behind_z, core)
    from_other = blocks(behind_y, behind_z, 1 - core)
    currents_ids = jnp.concatenate(
        [blocks(behind_y, turn, core), blocks(behind_y, turn, 1 - core)]
    )
    own = z[None]

    half = shape(16, scenarios, rows)
    waves = shape(3, scenarios, slots)
    splits = pltpu.VMEM((2 * scenarios, 16 * rows), BF16)
    end_split = pltpu.VMEM((2 * scenarios, ends), BF16)

    def spread(voltage_rows):
        column = jnp.stack(around(voltage_rows, "z"))
        plane = jnp.concatenate(around(column, "y"))
        return plane, swapped(plane)

    def first_gather(plane):
        return call(gather_kernel, (from_mine,), (terminal, plane), waves, [splits])

    def solve(h, other, step, voltage_rows):
        sent = swapped(other)
        mine = call(
            scatter_mine,
            (to_mine, own),
            (nodes, h, sources[step], fault, conductance, voltage_rows),
            half,
            [end_split],
        )
        quarters = call(
            join_kernel, (), (mine, sent), [shape(SIDE, scenarios, rows)] * SIDE
        )
        column = quarters[0]
        for k in range(1, SIDE):
            column = column + shifted(quarters[k], "y", k)
        total = sum(around(column, "z"))
        plane = jnp.concatenate(around(total, "y"))
        far = swapped(plane)
        block = shape(scenarios, rows)
        part = call(solve_first, (), (plane, inverse), block, [splits])
        return call(solve_rest, (), (far, inverse, part), block, [splits])

    voltage_rows = prior_voltage[0]
    plane, far = spread(voltage_rows)
    base, ka, e = fold(
        live_float,
        delay_steps,
        pole_wave[0],
        residue_wave[0],
        pole_admit[0],
        residue_admit[0],
        wave_state[0],
        admit_state[0],
        wave_history[0],
    )
    inverse = call(
        inverse_kernel,
        (currents_ids,),
        (conductance_inverse[0],),
        shape(2 * rows, node_count, dtype=BF16),
    )
    before = first_gather(plane)
    t0, h, other = call(
        first_kernel,
        (from_other, to_other),
        (terminal, nodes, far, before, base[0], ka[0]),
        (waves, waves, half),
        [splits, end_split],
    )
    voltage_rows = solve(h, other, 0, voltage_rows)
    terms = [t0]
    arrivals = []
    packed_shape = shape(devices, -(-CAPACITY * 3 * scenarios // 128) * 128)
    for step in range(1, STEPS):
        plane, far = spread(voltage_rows)
        before = first_gather(plane)
        term, packed = call(
            pack_kernel,
            (from_other,),
            (terminal, places, far, before, surge2, h),
            (waves, packed_shape),
            [splits],
        )
        terms.append(term)
        packed = lax.all_to_all(packed, NET_LINE, 0, 0, tiled=True)
        if step == 1:
            known = call(known_1, (), (base[1], ka, *terms), waves)
        else:
            known = call(known_2, (), (base[2], ka, *terms, e, arrivals[0]), waves)
        arrived, h, other = call(
            arrive_kernel,
            (to_other,),
            (nodes, places, packed, known, e),
            (waves, waves, half),
            [end_split],
        )
        arrivals.append(arrived)
        voltage_rows = solve(h, other, step, voltage_rows)
    plane, far = spread(voltage_rows)
    before = first_gather(plane)
    current = call(
        last_kernel, (from_other,), (terminal, far, before, surge, h), waves, [splits]
    )
    return voltage_rows[None], current[None]


def solution(mesh):
    finer = Mesh(mesh.devices.reshape(mesh.shape["net"], SIDE, SIDE, 2), NET_LINE)
    in_specs = (
        P("net", LINE, None),
        P("net", None, LINE),
        P(None, "net", LINE),
        P(),
        P(),
        P("net", None, LINE),
        P("net", LINE),
        P("net", LINE),
        P("net", LINE),
        P("net", LINE),
        P("net", None, LINE),
        P("net", None, None, None, LINE),
        P("net", None, LINE),
        P("net", None, None, None, LINE),
        P("net", None, None, None, LINE),
        P("net", None, None, None, LINE),
        P("net", None, None, None, LINE),
    )
    out_specs = (P("net", None, LINE), P("net", None, None, LINE))
    return jax.shard_map(
        on_device, mesh=finer, in_specs=in_specs, out_specs=out_specs, check_vma=False
    )
```

```python
import functools

import jax
import jax.numpy as jnp
from jax import lax
from jax.experimental import pallas as pl
from jax.experimental.pallas import tpu as pltpu
from jax.sharding import Mesh
from jax.sharding import PartitionSpec as P

STEPS = 3
LINE = ("z", "y", "core")
NET_LINE = ("net", "z", "y", "core")
SIDE = 4
CAPACITY = 5
F32 = jnp.float32
BF16 = jnp.bfloat16
VMEM = pl.BlockSpec(memory_space=pltpu.VMEM)
SMEM = pl.BlockSpec(memory_space=pltpu.SMEM)
FOLD_PARAMS = pltpu.CompilerParams(vmem_limit_bytes=56 * 1024 * 1024)
PARAMS = pltpu.CompilerParams(vmem_limit_bytes=32 * 1024 * 1024)


def shape(*dims, dtype=F32):
    return jax.ShapeDtypeStruct(dims, dtype)


def estimate(arrays, outs, flops):
    moved = sum(a.size * a.dtype.itemsize for a in [*arrays, *jax.tree.leaves(outs)])
    return pl.CostEstimate(flops=flops, bytes_accessed=moved, transcendentals=0)


def call(kernel, scalars, arrays, outs, scratch=(), flops=1_000_000):
    return pl.pallas_call(
        kernel,
        out_shape=outs,
        in_specs=[SMEM] * len(scalars) + [VMEM] * len(arrays),
        out_specs=jax.tree.map(lambda _: VMEM, outs),
        scratch_shapes=list(scratch),
        compiler_params=PARAMS,
        cost_estimate=estimate(arrays, outs, flops),
    )(*scalars, *arrays)


def halves(x):
    high = x.astype(BF16)
    low = (x - high.astype(F32)).astype(BF16)
    return high, low


def stacked(x):
    return jnp.concatenate(halves(x), axis=0)


def ones_where(mask):
    return jnp.where(mask, 1.0, 0.0).astype(BF16)


def dot(a, b, dims):
    return lax.dot_general(a, b, (dims, ((), ())), preferred_element_type=F32)


NN = ((1,), (0,))
NT = ((1,), (1,))
TN = ((0,), (0,))


def mix(coef, waves):
    return [
        coef[p, 0:1, :] * waves[0] + coef[p, 1:2, :] * waves[1] + coef[p, 2:3, :] * waves[2]
        for p in range(3)
    ]


def fold_kernel(own, delay, pw, rw, pa, ra, xw, xa, hist, h_out, ka_out, e_out):
    live = own[...]
    steps = delay[...]
    kw, ka = [], []
    for pole, res, into in ((pw, rw, kw), (pa, ra, ka)):
        for p in range(3):
            into.append([])
            power = None
            for m in range(STEPS):
                total = None
                for q in range(pole.shape[0]):
                    term = res[q, p]
                    for _ in range(m):
                        term = term * pole[q : q + 1, :]
                    total = term if total is None else total + term
                into[p].append(total * live)
    first = (steps == 1).astype(F32)
    second = (steps == 2).astype(F32)
    for p in range(3):
        for m in range(STEPS):
            ka_out[m, p] = ka[p][m]
        e_out[0, p] = kw[p][0] * first
        e_out[1, p] = kw[p][1] * first + kw[p][0] * second
    delayed = []
    for age in range(STEPS):
        rows = []
        for r in range(3):
            w = None
            for k in range(hist.shape[0] - age):
                part = jnp.where(steps == k + 1 + age, hist[k, r], 0.0)
                w = part if w is None else w + part
            rows.append(w)
        delayed.append(rows)
    for p in range(3):
        totals = [None] * STEPS
        for q in range(pw.shape[0]):
            w_pole = pw[q : q + 1, :]
            a_pole = pa[q : q + 1, :]
            w_now = xw[q, p]
            a_now = xa[q, p]
            for t in range(STEPS):
                w_now = w_now * w_pole
                a_now = a_now * a_pole
                part = w_now - a_now
                totals[t] = part if totals[t] is None else totals[t] + part
        for t in range(STEPS):
            value = totals[t] * live
            for s in range(t + 1):
                for r in range(3):
                    value = value + kw[p][t - s][r : r + 1, :] * delayed[s][r]
            h_out[t, p] = value


def fold(own, delay, pw, rw, pa, ra, xw, xa, hist):
    poles, _, scenarios, slots = xw.shape
    tile = 16
    whole = lambda *dims: pl.BlockSpec(dims, lambda i: (0,) * len(dims))
    state = pl.BlockSpec((poles, 3, tile, slots), lambda i: (0, 0, i, 0))
    arrays = (own, delay, pw, rw, pa, ra, xw, xa, hist)
    outs = (
        shape(STEPS, 3, scenarios, slots),
        shape(STEPS, 3, 3, slots),
        shape(2, 3, 3, slots),
    )
    return pl.pallas_call(
        fold_kernel,
        grid=(scenarios // tile,),
        out_shape=outs,
        in_specs=[
            whole(1, slots),
            whole(1, slots),
            whole(poles, slots),
            whole(poles, 3, 3, slots),
            whole(poles, slots),
            whole(poles, 3, 3, slots),
            state,
            state,
            pl.BlockSpec((hist.shape[0], 3, tile, slots), lambda i: (0, 0, i, 0)),
        ],
        out_specs=(
            pl.BlockSpec((STEPS, 3, tile, slots), lambda i: (0, 0, i, 0)),
            whole(STEPS, 3, 3, slots),
            whole(2, 3, 3, slots),
        ),
        compiler_params=FOLD_PARAMS,
        cost_estimate=estimate(arrays, outs, 30_000_000),
    )(*arrays)


def inverse_kernel(ids, inverse, out):
    rows = inverse.shape[0]
    for k in range(inverse.shape[1] // 128):
        block = inverse[:, pl.ds(pl.multiple_of(ids[k] * 128, 128), 128)]
        high, low = halves(block)
        out[0:rows, k * 128 : (k + 1) * 128] = high
        out[rows : 2 * rows, k * 128 : (k + 1) * 128] = low


def gather_into(ids, terminal, volts, split, emit):
    count, scenarios, lanes = volts.shape
    for k in range(count):
        high, low = halves(volts[k])
        split[0:scenarios, k * lanes : (k + 1) * lanes] = high
        split[scenarios : 2 * scenarios, k * lanes : (k + 1) * lanes] = low
    width = 256
    local = lax.broadcasted_iota(jnp.int32, (lanes, width), 0)
    for p in range(3):
        for n in range(terminal.shape[1] // width):
            cut = slice(n * width, (n + 1) * width)
            nodes = terminal[p : p + 1, cut]
            hot = jnp.concatenate(
                [ones_where(local == nodes - ids[k] * lanes) for k in range(count)], axis=0
            )
            both = dot(split[...], hot, NN)
            emit(p, cut, both[:scenarios] + both[scenarios:])


def gather_kernel(ids, terminal, volts, out, split):
    def emit(p, cut, value):
        out[p, :, cut] = value

    gather_into(ids, terminal, volts, split, emit)


def gather_rest(ids, terminal, volts, before, out, split):
    def emit(p, cut, value):
        out[p, :, cut] = before[p, :, cut] + value

    gather_into(ids, terminal, volts, split, emit)


def scatter_into(ids, nodes, split, emit):
    ends = split.shape[1]
    scenarios = split.shape[0] // 2
    local = lax.broadcasted_iota(jnp.int32, (128, ends), 0)
    for k in range(0, 16, 2):
        hot = jnp.concatenate(
            [ones_where(local == nodes - ids[k + i] * 128) for i in range(2)], axis=0
        )
        both = dot(split, hot, NT)
        value = both[:scenarios] + both[scenarios:]
        for i in range(2):
            emit(k + i, value[:, i * 128 : (i + 1) * 128])


def split_ends(h):
    parts = [stacked(h[p]) for p in range(3)]
    return jnp.concatenate(parts, axis=1)


def scatter_other(ids, nodes, h, out, split):
    def emit(k, value):
        out[k] = value

    split[...] = split_ends(h)
    scatter_into(ids, nodes[...], split[...], emit)


def first_kernel(ids, to, terminal, nodes, volts, before, base, ka, term, h_out, out, split, ends):
    gather_rest(ids, terminal, volts, before, term, split)
    drop = mix(ka, term)
    for p in range(3):
        h_out[p] = base[p] - drop[p]
    scatter_other(to, nodes, h_out, out, ends)


def scatter_mine(ids, own, nodes, h, source, fault, conductance, volts, out, split):
    def emit(k, value):
        out[k] = value

    split[...] = split_ends(h)
    scatter_into(ids, nodes[...], split[...], emit)
    lane = lax.broadcasted_iota(jnp.int32, volts.shape, 1)
    drawn = jnp.where(lane == fault[...], conductance[...] * volts[...], 0.0)
    me = own[0]
    out[me] = out[me] + source[...] - drawn


def hot_places(places, count):
    owner = lax.broadcasted_iota(jnp.int32, (count, places.shape[1]), 0)
    return [ones_where(owner * 8 + r == places) for r in range(CAPACITY)]


def packed_lines(values):
    return -(-CAPACITY * values // 128)


def pack_kernel(ids, terminal, places, volts, before, surge2, h, term, packed, split):
    gather_rest(ids, terminal, volts, before, term, split)
    waves = [surge2[...] * term[p] - h[p] for p in range(3)]
    high, low = halves(jnp.concatenate(waves, axis=0))
    lines = packed_lines(high.shape[0])
    owners = packed.shape[0] // lines
    rows = []
    for hot in hot_places(places[...], owners):
        rows.append(dot(hot, high, NT) + dot(hot, low, NT))
    used = sum(r.shape[1] for r in rows)
    rows.append(jnp.zeros((owners, lines * 128 - used), F32))
    rows = jnp.concatenate(rows, axis=1)
    for k in range(lines):
        packed[pl.ds(k, owners, stride=lines), :] = rows[:, k * 128 : (k + 1) * 128]


def known_1(base, ka, t0, t1, out):
    a, b = mix(ka[1], t0), mix(ka[0], t1)
    for p in range(3):
        out[p] = base[p] - a[p] - b[p]


def known_2(base, ka, t0, t1, t2, e, a1, out):
    a, b, c, d = mix(ka[2], t0), mix(ka[1], t1), mix(ka[0], t2), mix(e[1], a1)
    for p in range(3):
        out[p] = base[p] - a[p] - b[p] - c[p] + d[p]


def arrive_kernel(to, nodes, places, packed, base, e, arrived, h_out, out, ends):
    scenarios = base.shape[1]
    wide = 3 * scenarios
    lines = packed_lines(wide)
    owners = packed.shape[0] // lines
    rows = jnp.concatenate(
        [packed[pl.ds(k, owners, stride=lines), :] for k in range(lines)], axis=1
    )
    total = None
    for r, hot in enumerate(hot_places(places[...], owners)):
        high, low = halves(rows[:, r * wide : (r + 1) * wide])
        part = dot(high, hot, TN) + dot(low, hot, TN)
        total = part if total is None else total + part
    for p in range(3):
        arrived[p] = total[p * scenarios : (p + 1) * scenarios]
    gain = mix(e[0], arrived)
    for p in range(3):
        h_out[p] = base[p] + gain[p]
    scatter_other(to, nodes, h_out, out, ends)


def last_kernel(ids, terminal, volts, before, surge, h, out, split):
    def emit(p, cut, value):
        term = before[p, :, cut] + value
        out[p, :, cut] = surge[:, cut] * term - h[p, :, cut]

    gather_into(ids, terminal, volts, split, emit)


def join_kernel(mine, other, *outs):
    for k, out in enumerate(outs):
        for z in range(SIDE):
            out[z] = mine[k * SIDE + z] + other[k * SIDE + z]


def solve_into(current, inverse, part, split):
    count, scenarios, lanes = current.shape
    for k in range(count):
        high, low = halves(current[k])
        split[0:scenarios, k * lanes : (k + 1) * lanes] = high
        split[scenarios : 2 * scenarios, k * lanes : (k + 1) * lanes] = low
    width = count * lanes
    both = dot(split[...], inverse[:, part * width : (part + 1) * width], NT)
    return both[:scenarios, :lanes] + both[:scenarios, lanes:] + both[scenarios:, :lanes]


def solve_first(current, inverse, out, split):
    out[...] = solve_into(current, inverse, 0, split)


def solve_rest(current, inverse, before, out, split):
    out[...] = before[...] + solve_into(current, inverse, 1, split)


def collect_kernel(*refs):
    out = refs[-1]
    for k, ref in enumerate(refs[:-1]):
        if len(ref.shape) == len(out.shape):
            out[k * ref.shape[0] : (k + 1) * ref.shape[0]] = ref[...]
        else:
            out[k] = ref[...]


def shifted(x, axis, shift):
    return lax.ppermute(x, axis, [(i, (i + shift) % SIDE) for i in range(SIDE)])


def swapped(x):
    return lax.ppermute(x, "core", [(0, 1), (1, 0)])


def around(x, axis):
    return [x] + [shifted(x, axis, k) for k in range(1, SIDE)]


def on_device(
    conductance_inverse,
    prior_voltage,
    sources,
    fault_node,
    fault_conductance,
    terminal_node,
    ownership,
    partner,
    delay_steps,
    surge_conductance,
    pole_wave,
    residue_wave,
    pole_admit,
    residue_admit,
    wave_state,
    admit_state,
    wave_history,
):
    rows, node_count = conductance_inverse.shape[1:]
    scenarios = prior_voltage.shape[1]
    slots = ownership.shape[1]
    ends = 3 * slots
    devices = lax.axis_size(NET_LINE)
    net, z, y, core = (lax.axis_index(a) for a in NET_LINE)
    me = lax.axis_index(LINE)

    live = ownership[0] > 0
    live_float = live.astype(F32)[None]
    partners = partner[0]
    slot = jnp.arange(slots, dtype=jnp.int32)
    earlier = (
        (partners[:, None] == partners[None, :])
        & live[:, None]
        & (slot[:, None] < slot[None, :])
    )
    rank = jnp.sum(earlier.astype(jnp.int32), axis=0)
    places = jnp.where(live, partners * 8 + rank, -1)[None]
    terminal = terminal_node[0]
    nodes = terminal.reshape(1, ends)
    surge = surge_conductance * live_float
    surge2 = 2.0 * surge
    fault = (fault_node - (net * node_count + me * rows))[:, None]
    conductance = fault_conductance[:, None]

    turn = jnp.arange(SIDE, dtype=jnp.int32)
    behind_z, behind_y = (z - turn) % SIDE, (y - turn) % SIDE

    def blocks(ys, zs, c):
        return ((zs[None, :] * SIDE + ys[:, None]) * 2 + c).reshape(-1)

    to_mine = blocks((y + turn) % SIDE, turn, core)
    to_other = blocks((y + turn) % SIDE, turn, 1 - core)
    from_mine = blocks(behind_y, behind_z, core)
    from_other = blocks(behind_y, behind_z, 1 - core)
    currents_ids = jnp.concatenate(
        [blocks(behind_y, turn, core), blocks(behind_y, turn, 1 - core)]
    )
    own = z[None]

    half = shape(16, scenarios, rows)
    waves = shape(3, scenarios, slots)
    splits = pltpu.VMEM((2 * scenarios, 16 * rows), BF16)
    end_split = pltpu.VMEM((2 * scenarios, ends), BF16)

    def spread(voltage_rows):
        column = call(
            collect_kernel, (), around(voltage_rows, "z"), shape(SIDE, scenarios, rows)
        )
        plane = call(collect_kernel, (), around(column, "y"), half)
        return plane, swapped(plane)

    def first_gather(plane):
        return call(gather_kernel, (from_mine,), (terminal, plane), waves, [splits])

    def solve(h, other, step, voltage_rows):
        sent = swapped(other)
        mine = call(
            scatter_mine,
            (to_mine, own),
            (nodes, h, sources[step], fault, conductance, voltage_rows),
            half,
            [end_split],
        )
        quarters = call(
            join_kernel, (), (mine, sent), [shape(SIDE, scenarios, rows)] * SIDE
        )
        column = quarters[0]
        for k in range(1, SIDE):
            column = column + shifted(quarters[k], "y", k)
        total = sum(around(column, "z"))
        plane = call(collect_kernel, (), around(total, "y"), half)
        far = swapped(plane)
        block = shape(scenarios, rows)
        part = call(solve_first, (), (plane, inverse), block, [splits])
        return call(solve_rest, (), (far, inverse, part), block, [splits])

    voltage_rows = prior_voltage[0]
    plane, far = spread(voltage_rows)
    base, ka, e = fold(
        live_float,
        delay_steps,
        pole_wave[0],
        residue_wave[0],
        pole_admit[0],
        residue_admit[0],
        wave_state[0],
        admit_state[0],
        wave_history[0],
    )
    inverse = call(
        inverse_kernel,
        (currents_ids,),
        (conductance_inverse[0],),
        shape(2 * rows, node_count, dtype=BF16),
    )
    before = first_gather(plane)
    t0, h, other = call(
        first_kernel,
        (from_other, to_other),
        (terminal, nodes, far, before, base[0], ka[0]),
        (waves, waves, half),
        [splits, end_split],
    )
    voltage_rows = solve(h, other, 0, voltage_rows)
    terms = [t0]
    arrivals = []
    lines = packed_lines(3 * scenarios)
    packed_shape = shape(devices * lines, 128)
    for step in range(1, STEPS):
        plane, far = spread(voltage_rows)
        before = first_gather(plane)
        term, packed = call(
            pack_kernel,
            (from_other,),
            (terminal, places, far, before, surge2, h),
            (waves, packed_shape),
            [splits],
        )
        terms.append(term)
        packed = packed.reshape(devices, 1, lines * 128)
        packed = lax.all_to_all(packed, NET_LINE, 0, 0, tiled=True)
        packed = packed.reshape(devices * lines, 128)
        if step == 1:
            known = call(known_1, (), (base[1], ka, *terms), waves)
        else:
            known = call(known_2, (), (base[2], ka, *terms, e, arrivals[0]), waves)
        arrived, h, other = call(
            arrive_kernel,
            (to_other,),
            (nodes, places, packed, known, e),
            (waves, waves, half),
            [end_split],
        )
        arrivals.append(arrived)
        voltage_rows = solve(h, other, step, voltage_rows)
    plane, far = spread(voltage_rows)
    before = first_gather(plane)
    current = call(
        last_kernel, (from_other,), (terminal, far, before, surge, h), waves, [splits]
    )
    return voltage_rows[None], current[None]


def solution(mesh):
    finer = Mesh(mesh.devices.reshape(mesh.shape["net"], SIDE, SIDE, 2), NET_LINE)
    in_specs = (
        P("net", LINE, None),
        P("net", None, LINE),
        P(None, "net", LINE),
        P(),
        P(),
        P("net", None, LINE),
        P("net", LINE),
        P("net", LINE),
        P("net", LINE),
        P("net", LINE),
        P("net", None, LINE),
        P("net", None, None, None, LINE),
        P("net", None, LINE),
        P("net", None, None, None, LINE),
        P("net", None, None, None, LINE),
        P("net", None, None, None, LINE),
        P("net", None, None, None, LINE),
    )
    out_specs = (P("net", None, LINE), P("net", None, None, LINE))
    return jax.shard_map(
        on_device, mesh=finer, in_specs=in_specs, out_specs=out_specs, check_vma=False
    )
```

```python
import functools

import jax
import jax.numpy as jnp
from jax import lax
from jax.experimental import pallas as pl
from jax.experimental.pallas import tpu as pltpu
from jax.sharding import Mesh
from jax.sharding import PartitionSpec as P

STEPS = 3
PLANE = ("z", "y")
LINE = ("z", "y", "core")
NET_LINE = ("net", "z", "y", "core")
SIDE = 4
CHIPS = SIDE * SIDE
CAPACITY = 5
F32 = jnp.float32
BF16 = jnp.bfloat16
VMEM = pl.BlockSpec(memory_space=pltpu.VMEM)
SMEM = pl.BlockSpec(memory_space=pltpu.SMEM)
PARAMS = pltpu.CompilerParams(vmem_limit_bytes=16 * 1024 * 1024)


def shape(*dims, dtype=F32):
    return jax.ShapeDtypeStruct(dims, dtype)


def estimate(arrays, outs, flops):
    moved = sum(a.size * a.dtype.itemsize for a in [*arrays, *jax.tree.leaves(outs)])
    return pl.CostEstimate(flops=flops, bytes_accessed=moved, transcendentals=0)


def call(kernel, scalars, arrays, outs, scratch=(), flops=1_000_000):
    return pl.pallas_call(
        kernel,
        out_shape=outs,
        in_specs=[SMEM] * len(scalars) + [VMEM] * len(arrays),
        out_specs=jax.tree.map(lambda _: VMEM, outs),
        scratch_shapes=list(scratch),
        compiler_params=PARAMS,
        cost_estimate=estimate(arrays, outs, flops),
    )(*scalars, *arrays)


def halves(x):
    high = x.astype(BF16)
    low = (x - high.astype(F32)).astype(BF16)
    return high, low


def stacked(x):
    return jnp.concatenate(halves(x), axis=0)


def ones_where(mask):
    return jnp.where(mask, 1.0, 0.0).astype(BF16)


def dot(a, b, dims):
    return lax.dot_general(a, b, (dims, ((), ())), preferred_element_type=F32)


NN = ((1,), (0,))
NT = ((1,), (1,))
TN = ((0,), (0,))


def mix(coef, waves):
    return [
        coef[p, 0:1, :] * waves[0] + coef[p, 1:2, :] * waves[1] + coef[p, 2:3, :] * waves[2]
        for p in range(3)
    ]


def fold_kernel(own, delay, pw, rw, pa, ra, xw, xa, hist, h0, h1, h2, coef_out):
    h_out = (h0, h1, h2)
    live = own[...]
    steps = delay[...]
    kw, ka = [], []
    for pole, res, into in ((pw, rw, kw), (pa, ra, ka)):
        for p in range(3):
            into.append([])
            power = None
            for m in range(STEPS):
                total = None
                for q in range(pole.shape[0]):
                    term = res[q, p]
                    for _ in range(m):
                        term = term * pole[q : q + 1, :]
                    total = term if total is None else total + term
                into[p].append(total * live)
    first = (steps == 1).astype(F32)
    second = (steps == 2).astype(F32)
    for p in range(3):
        for m in range(STEPS):
            coef_out[m, p] = ka[p][m]
        coef_out[STEPS, p] = kw[p][0] * first
        coef_out[STEPS + 1, p] = kw[p][1] * first + kw[p][0] * second
    delayed = []
    for age in range(STEPS):
        rows = []
        for r in range(3):
            w = None
            for k in range(hist.shape[0] - age):
                part = jnp.where(steps == k + 1 + age, hist[k, r], 0.0)
                w = part if w is None else w + part
            rows.append(w)
        delayed.append(rows)
    for p in range(3):
        totals = [None] * STEPS
        for q in range(pw.shape[0]):
            w_pole = pw[q : q + 1, :]
            a_pole = pa[q : q + 1, :]
            w_now = xw[q, p]
            a_now = xa[q, p]
            for t in range(STEPS):
                w_now = w_now * w_pole
                a_now = a_now * a_pole
                part = w_now - a_now
                totals[t] = part if totals[t] is None else totals[t] + part
        for t in range(STEPS):
            value = totals[t] * live
            for s in range(t + 1):
                for r in range(3):
                    value = value + kw[p][t - s][r : r + 1, :] * delayed[s][r]
            h_out[t][p] = value


def fold(own, delay, pw, rw, pa, ra, xw, xa, hist):
    poles, _, scenarios, slots = xw.shape
    tile = 16
    whole = lambda *dims: pl.BlockSpec(dims, lambda i: (0,) * len(dims))
    state = pl.BlockSpec((poles, 3, tile, slots), lambda i: (0, 0, i, 0))
    arrays = (own, delay, pw, rw, pa, ra, xw, xa, hist)
    outs = (
        *[shape(3, scenarios, slots)] * STEPS,
        shape(STEPS + 2, 3, 3, slots),
    )
    return pl.pallas_call(
        fold_kernel,
        grid=(scenarios // tile,),
        out_shape=outs,
        in_specs=[
            whole(1, slots),
            whole(1, slots),
            whole(poles, slots),
            whole(poles, 3, 3, slots),
            whole(poles, slots),
            whole(poles, 3, 3, slots),
            state,
            state,
            pl.BlockSpec((hist.shape[0], 3, tile, slots), lambda i: (0, 0, i, 0)),
        ],
        out_specs=(
            *[pl.BlockSpec((3, tile, slots), lambda i: (0, i, 0))] * STEPS,
            whole(STEPS + 2, 3, 3, slots),
        ),
        compiler_params=PARAMS,
        cost_estimate=estimate(arrays, outs, 30_000_000),
    )(*arrays)


def inverse_kernel(pos, inverse, out):
    rows = inverse.shape[0]
    for k in range(2 * CHIPS):
        side = pos[0] if k < CHIPS else 1 - pos[0]
        start = pl.multiple_of(((k % CHIPS) * 2 + side) * 128, 128)
        block = inverse[:, pl.ds(start, 128)]
        high, low = halves(block)
        out[0:rows, k * 128 : (k + 1) * 128] = high
        out[rows : 2 * rows, k * 128 : (k + 1) * 128] = low


def gather_into(side, terminal, volts, split, emit):
    count, scenarios, lanes = volts.shape
    for k in range(count):
        high, low = halves(volts[k])
        split[0:scenarios, k * lanes : (k + 1) * lanes] = high
        split[scenarios : 2 * scenarios, k * lanes : (k + 1) * lanes] = low
    width = 256
    local = lax.broadcasted_iota(jnp.int32, (lanes, width), 0)
    for p in range(3):
        for n in range(terminal.shape[1] // width):
            cut = slice(n * width, (n + 1) * width)
            nodes = terminal[p : p + 1, cut]
            hot = jnp.concatenate(
                [ones_where(local == nodes - (2 * k + side) * lanes) for k in range(count)], axis=0
            )
            both = dot(split[...], hot, NN)
            emit(p, cut, both[:scenarios] + both[scenarios:])


def gather_kernel(pos, terminal, volts, out, split):
    def emit(p, cut, value):
        out[p, :, cut] = value

    gather_into(pos[0], terminal, volts, split, emit)


def gather_rest(pos, terminal, volts, before, out, split):
    def emit(p, cut, value):
        out[p, :, cut] = before[p, :, cut] + value

    gather_into(1 - pos[0], terminal, volts, split, emit)


def scatter_into(side, terminal, split, emit):
    ends = split.shape[1]
    scenarios = split.shape[0] // 2
    local = lax.broadcasted_iota(jnp.int32, (128, ends), 0)
    nodes = jnp.concatenate([terminal[p : p + 1, :] for p in range(3)], axis=1)
    for k in range(0, CHIPS, 2):
        hot = jnp.concatenate(
            [ones_where(local == nodes - (2 * (k + i) + side) * 128) for i in range(2)], axis=0
        )
        both = dot(split, hot, NT)
        value = both[:scenarios] + both[scenarios:]
        for i in range(2):
            emit(k + i, value[:, i * 128 : (i + 1) * 128])


def split_ends(h):
    parts = [stacked(h[p]) for p in range(3)]
    return jnp.concatenate(parts, axis=1)


def scatter_other(pos, terminal, h, out, split):
    def emit(k, value):
        out[k] = value

    split[...] = split_ends(h)
    scatter_into(1 - pos[0], terminal, split[...], emit)


def first_kernel(pos, terminal, volts, before, base, coef, term, h_out, out, split, ends):
    gather_rest(pos, terminal, volts, before, term, split)
    drop = mix(coef[0], term)
    for p in range(3):
        h_out[p] = base[p] - drop[p]
    scatter_other(pos, terminal, h_out, out, ends)


def scatter_mine(step, pos, terminal, h, source, drain, volts, out, split):
    def emit(k, value):
        out[k] = value

    split[...] = split_ends(h)
    scatter_into(pos[0], terminal, split[...], emit)
    me = pos[1]
    out[me] = out[me] + source[step] - drain[...] * volts[...]


def hot_places(places, count):
    owner = lax.broadcasted_iota(jnp.int32, (count, places.shape[1]), 0)
    return [ones_where(owner * 8 + r == places) for r in range(CAPACITY)]


def packed_lines(values):
    return -(-CAPACITY * values // 128)


def pack_kernel(pos, terminal, places, volts, before, surge2, h, term, packed, split):
    gather_rest(pos, terminal, volts, before, term, split)
    waves = [surge2[...] * term[p] - h[p] for p in range(3)]
    high, low = halves(jnp.concatenate(waves, axis=0))
    lines = packed_lines(high.shape[0])
    owners = packed.shape[0] // lines
    rows = []
    for hot in hot_places(places[...], owners):
        rows.append(dot(hot, high, NT) + dot(hot, low, NT))
    used = sum(r.shape[1] for r in rows)
    rows.append(jnp.zeros((owners, lines * 128 - used), F32))
    rows = jnp.concatenate(rows, axis=1)
    for k in range(lines):
        packed[pl.ds(k, owners, stride=lines), :] = rows[:, k * 128 : (k + 1) * 128]


def known_1(base, coef, t0, t1, out):
    a, b = mix(coef[1], t0), mix(coef[0], t1)
    for p in range(3):
        out[p] = base[p] - a[p] - b[p]


def known_2(base, coef, t0, t1, t2, a1, out):
    a, b, c = mix(coef[2], t0), mix(coef[1], t1), mix(coef[0], t2)
    d = mix(coef[STEPS + 1], a1)
    for p in range(3):
        out[p] = base[p] - a[p] - b[p] - c[p] + d[p]


def arrive_kernel(pos, terminal, places, packed, base, coef, arrived, h_out, out, ends):
    scenarios = base.shape[1]
    wide = 3 * scenarios
    lines = packed_lines(wide)
    owners = packed.shape[0] // lines
    rows = jnp.concatenate(
        [packed[pl.ds(k, owners, stride=lines), :] for k in range(lines)], axis=1
    )
    total = None
    for r, hot in enumerate(hot_places(places[...], owners)):
        high, low = halves(rows[:, r * wide : (r + 1) * wide])
        part = dot(high, hot, TN) + dot(low, hot, TN)
        total = part if total is None else total + part
    for p in range(3):
        arrived[p] = total[p * scenarios : (p + 1) * scenarios]
    gain = mix(coef[STEPS], arrived)
    for p in range(3):
        h_out[p] = base[p] + gain[p]
    scatter_other(pos, terminal, h_out, out, ends)


def last_kernel(pos, terminal, volts, before, surge, h, out, split):
    def emit(p, cut, value):
        term = before[p, :, cut] + value
        out[p, :, cut] = surge[:, cut] * term - h[p, :, cut]

    gather_into(1 - pos[0], terminal, volts, split, emit)


def total_kernel(parts, out):
    total = parts[0]
    for k in range(1, CHIPS):
        total = total + parts[k]
    for k in range(CHIPS):
        out[k] = total


def solve_into(current, inverse, part, split):
    count, scenarios, lanes = current.shape
    for k in range(count):
        high, low = halves(current[k])
        split[0:scenarios, k * lanes : (k + 1) * lanes] = high
        split[scenarios : 2 * scenarios, k * lanes : (k + 1) * lanes] = low
    width = count * lanes
    both = dot(split[...], inverse[:, part * width : (part + 1) * width], NT)
    return both[:scenarios, :lanes] + both[:scenarios, lanes:] + both[scenarios:, :lanes]


def solve_first(current, inverse, out, split):
    out[...] = solve_into(current, inverse, 0, split)


def solve_rest(current, inverse, before, rows, out, split):
    volts = before[...] + solve_into(current, inverse, 1, split)
    rows[...] = volts
    for k in range(CHIPS):
        out[k] = volts


def exchanged(x):
    return lax.all_to_all(x, PLANE, 0, 0, tiled=True)


def swapped(x):
    return lax.ppermute(x, "core", [(0, 1), (1, 0)])


def on_device(
    conductance_inverse,
    prior_voltage,
    sources,
    fault_node,
    fault_conductance,
    terminal_node,
    ownership,
    partner,
    delay_steps,
    surge_conductance,
    pole_wave,
    residue_wave,
    pole_admit,
    residue_admit,
    wave_state,
    admit_state,
    wave_history,
):
    rows, node_count = conductance_inverse.shape[1:]
    scenarios = prior_voltage.shape[1]
    slots = ownership.shape[1]
    ends = 3 * slots
    devices = lax.axis_size(NET_LINE)
    net, z, y, core = (lax.axis_index(a) for a in NET_LINE)
    me = lax.axis_index(LINE)

    live = ownership[0] > 0
    live_float = live.astype(F32)[None]
    partners = partner[0]
    slot = jnp.arange(slots, dtype=jnp.int32)
    earlier = (
        (partners[:, None] == partners[None, :])
        & live[:, None]
        & (slot[:, None] < slot[None, :])
    )
    rank = jnp.sum(earlier.astype(jnp.int32), axis=0)
    places = jnp.where(live, partners * 8 + rank, -1)[None]
    terminal = terminal_node[0]
    surge = surge_conductance * live_float
    surge2 = 2.0 * surge
    lane = jnp.arange(rows, dtype=jnp.int32)[None]
    first_node = net * node_count + me * rows
    drain = jnp.where(
        fault_node[:, None] - first_node == lane, fault_conductance[:, None], 0.0
    )
    pos = jnp.stack([core, z * SIDE + y]).astype(jnp.int32)

    half = shape(CHIPS, scenarios, rows)
    waves = shape(3, scenarios, slots)
    splits = pltpu.VMEM((2 * scenarios, 16 * rows), BF16)
    end_split = pltpu.VMEM((2 * scenarios, ends), BF16)

    block = shape(scenarios, rows)

    def first_gather(plane):
        return call(gather_kernel, (pos,), (terminal, plane), waves, [splits], 4_000_000_000)

    def solve(h, other, step, voltage_rows):
        sent = swapped(other)
        mine = call(
            functools.partial(scatter_mine, step),
            (pos,),
            (terminal, h, sources, drain, voltage_rows),
            half,
            [end_split],
            4_000_000_000,
        )
        plane = exchanged(call(total_kernel, (), (exchanged(mine + sent),), half))
        far = swapped(plane)
        part = call(solve_first, (), (plane, inverse), block, [splits], 500_000_000)
        return call(solve_rest, (), (far, inverse, part), (block, half), [splits], 500_000_000)

    voltage_rows = prior_voltage[0]
    plane = exchanged(jnp.broadcast_to(voltage_rows[None], half.shape))
    *base, coef = fold(
        live_float,
        delay_steps,
        pole_wave[0],
        residue_wave[0],
        pole_admit[0],
        residue_admit[0],
        wave_state[0],
        admit_state[0],
        wave_history[0],
    )
    inverse = call(
        inverse_kernel,
        (pos,),
        (conductance_inverse[0],),
        shape(2 * rows, node_count, dtype=BF16),
    )
    plane, base, coef, inverse = lax.optimization_barrier((plane, base, coef, inverse))
    far = swapped(plane)
    before = first_gather(plane)
    t0, h, other = call(
        first_kernel,
        (pos,),
        (terminal, far, before, base[0], coef),
        (waves, waves, half),
        [splits, end_split],
        8_000_000_000,
    )
    voltage_rows, copies = solve(h, other, 0, voltage_rows)
    terms = [t0]
    arrivals = []
    lines = packed_lines(3 * scenarios)
    packed_shape = shape(devices * lines, 128)
    for step in range(1, STEPS):
        plane = exchanged(copies)
        far = swapped(plane)
        before = first_gather(plane)
        term, packed = call(
            pack_kernel,
            (pos,),
            (terminal, places, far, before, surge2, h),
            (waves, packed_shape),
            [splits],
            5_000_000_000,
        )
        terms.append(term)
        packed = packed.reshape(devices, 1, lines * 128)
        packed = lax.all_to_all(packed, NET_LINE, 0, 0, tiled=True)
        packed = packed.reshape(devices * lines, 128)
        known = call((known_1, known_2)[step - 1], (), (base[step], coef, *terms, *arrivals), waves)
        arrived, h, other = call(
            arrive_kernel,
            (pos,),
            (terminal, places, packed, known, coef),
            (waves, waves, half),
            [end_split],
            5_000_000_000,
        )
        arrivals.append(arrived)
        voltage_rows, copies = solve(h, other, step, voltage_rows)
    plane = exchanged(copies)
    far = swapped(plane)
    before = first_gather(plane)
    current = call(
        last_kernel, (pos,), (terminal, far, before, surge, h), waves, [splits], 4_000_000_000
    )
    return voltage_rows[None], current[None]


def solution(mesh):
    finer = Mesh(mesh.devices.reshape(mesh.shape["net"], SIDE, SIDE, 2), NET_LINE)
    in_specs = (
        P("net", LINE, None),
        P("net", None, LINE),
        P(None, "net", LINE),
        P(),
        P(),
        P("net", None, LINE),
        P("net", LINE),
        P("net", LINE),
        P("net", LINE),
        P("net", LINE),
        P("net", None, LINE),
        P("net", None, None, None, LINE),
        P("net", None, LINE),
        P("net", None, None, None, LINE),
        P("net", None, None, None, LINE),
        P("net", None, None, None, LINE),
        P("net", None, None, None, LINE),
    )
    out_specs = (P("net", None, LINE), P("net", None, None, LINE))
    return jax.shard_map(
        on_device, mesh=finer, in_specs=in_specs, out_specs=out_specs, check_vma=False
    )
```

```python
import functools

import jax
import jax.numpy as jnp
from jax import lax
from jax.experimental import pallas as pl
from jax.experimental.pallas import tpu as pltpu
from jax.sharding import Mesh
from jax.sharding import PartitionSpec as P

STEPS = 3
PLANE = ("z", "y")
LINE = ("z", "y", "core")
NET_LINE = ("net", "z", "y", "core")
SIDE = 4
CHIPS = SIDE * SIDE
CAPACITY = 5
F32 = jnp.float32
BF16 = jnp.bfloat16
VMEM = pl.BlockSpec(memory_space=pltpu.VMEM)
SMEM = pl.BlockSpec(memory_space=pltpu.SMEM)
PARAMS = pltpu.CompilerParams(vmem_limit_bytes=16 * 1024 * 1024)


def shape(*dims, dtype=F32):
    return jax.ShapeDtypeStruct(dims, dtype)


def estimate(arrays, outs, flops):
    moved = sum(a.size * a.dtype.itemsize for a in [*arrays, *jax.tree.leaves(outs)])
    return pl.CostEstimate(flops=flops, bytes_accessed=moved, transcendentals=0)


def call(kernel, scalars, arrays, outs, scratch=(), flops=1_000_000):
    return pl.pallas_call(
        kernel,
        out_shape=outs,
        in_specs=[SMEM] * len(scalars) + [VMEM] * len(arrays),
        out_specs=jax.tree.map(lambda _: VMEM, outs),
        scratch_shapes=list(scratch),
        compiler_params=PARAMS,
        cost_estimate=estimate(arrays, outs, flops),
    )(*scalars, *arrays)


def halves(x):
    high = x.astype(BF16)
    low = (x - high.astype(F32)).astype(BF16)
    return high, low


def stacked(x):
    return jnp.concatenate(halves(x), axis=0)


def ones_where(mask):
    return jnp.where(mask, 1.0, 0.0).astype(BF16)


def within_block(nodes, block):
    return jnp.clip(nodes - block * 128, -1, 128).astype(F32).astype(BF16)


def hot_block(local, nodes, block):
    one, zero = jnp.ones((), BF16), jnp.zeros((), BF16)
    return jnp.where(local == within_block(nodes, block), one, zero)


def block_places(width):
    return lax.broadcasted_iota(jnp.int32, (128, width), 0).astype(F32).astype(BF16)


def dot(a, b, dims):
    return lax.dot_general(a, b, (dims, ((), ())), preferred_element_type=F32)


NN = ((1,), (0,))
NT = ((1,), (1,))
TN = ((0,), (0,))


def mix(coef, waves):
    return [
        coef[p, 0:1, :] * waves[0] + coef[p, 1:2, :] * waves[1] + coef[p, 2:3, :] * waves[2]
        for p in range(3)
    ]


def lag_coefficients(own, delay, pw, rw, pa, ra, coef):
    live = own[...]
    steps = delay[...]
    first = (steps == 1).astype(F32)
    second = (steps == 2).astype(F32)
    for p in range(3):
        lags = []
        for pole, res in ((pa, ra), (pw, rw)):
            terms = [res[q, p] for q in range(pole.shape[0])]
            for m in range(STEPS):
                if m:
                    terms = [x * pole[q : q + 1, :] for q, x in enumerate(terms)]
                lags.append(sum(terms[1:], terms[0]) * live)
        for m in range(STEPS):
            coef[m, p] = lags[m]
            coef[STEPS + 2 + m, p] = lags[STEPS + m]
        coef[STEPS, p] = lags[STEPS] * first
        coef[STEPS + 1, p] = lags[STEPS + 1] * first + lags[STEPS] * second


def fold_states(times, own, delay, pw, pa, coef, xw, xa, hist, outs):
    live = own[...]
    steps = delay[...]
    delayed = []
    for age in range(max(times) + 1):
        rows = []
        for r in range(3):
            w = None
            for k in range(hist.shape[0] - age):
                part = jnp.where(steps == k + 1 + age, hist[k, r], 0.0)
                w = part if w is None else w + part
            rows.append(w)
        delayed.append(rows)
    for p in range(3):
        totals = {}
        for q in range(pw.shape[0]):
            w_now = xw[q, p]
            a_now = xa[q, p]
            for t in range(max(times) + 1):
                w_now = w_now * pw[q : q + 1, :]
                a_now = a_now * pa[q : q + 1, :]
                if t in times:
                    part = w_now - a_now
                    totals[t] = totals[t] + part if t in totals else part
        for t, out in zip(times, outs):
            value = totals[t] * live
            for s in range(t + 1):
                lag = STEPS + 2 + t - s
                for r in range(3):
                    value = value + coef[lag, p, r : r + 1, :] * delayed[s][r]
            out[p] = value


def fold_first(own, delay, pw, rw, pa, ra, xw, xa, hist, out, coef):
    @pl.when(pl.program_id(0) == 0)
    def _():
        lag_coefficients(own, delay, pw, rw, pa, ra, coef)

    fold_states((0,), own, delay, pw, pa, coef, xw, xa, hist, (out,))


def fold_later(own, delay, pw, pa, coef, xw, xa, hist, *outs):
    fold_states((1, 2), own, delay, pw, pa, coef, xw, xa, hist, outs)


def fold(kernel, small, states, bases, coefs):
    poles, _, scenarios, slots = states[0].shape
    tile = 16
    whole = lambda a: pl.BlockSpec(a.shape, lambda i: (0,) * len(a.shape))
    cut = lambda a: pl.BlockSpec((*a.shape[:2], tile, slots), lambda i: (0, 0, i, 0))
    out = shape(3, scenarios, slots)
    outs = [out] * bases + coefs
    return pl.pallas_call(
        kernel,
        grid=(scenarios // tile,),
        out_shape=outs,
        in_specs=[whole(a) for a in small] + [cut(a) for a in states],
        out_specs=[pl.BlockSpec((3, tile, slots), lambda i: (0, i, 0))] * bases
        + [whole(a) for a in coefs],
        compiler_params=PARAMS,
        cost_estimate=estimate((*small, *states), outs, 20_000_000),
    )(*small, *states)


def cut_kernel(pos, inverse, mine, give):
    rows = inverse.shape[0]
    for k in range(CHIPS):
        lanes = slice(k * 128, (k + 1) * 128)
        start = pl.multiple_of((k * 2 + pos[0]) * 128, 128)
        high, low = halves(inverse[:, pl.ds(start, 128)])
        mine[0:rows, lanes] = high
        mine[rows : 2 * rows, lanes] = low
        start = pl.multiple_of((k * 2 + 1 - pos[0]) * 128, 128)
        give[:, lanes] = inverse[:, pl.ds(start, 128)]


def split_kernel(inverse, out):
    rows = inverse.shape[0]
    high, low = halves(inverse[...])
    out[0:rows] = high
    out[rows : 2 * rows] = low


def gather_into(side, terminal, volts, split, emit):
    count, scenarios, lanes = volts.shape
    for k in range(count):
        high, low = halves(volts[k])
        split[0:scenarios, k * lanes : (k + 1) * lanes] = high
        split[scenarios : 2 * scenarios, k * lanes : (k + 1) * lanes] = low
    width = 256
    local = block_places(width)
    for p in range(3):
        for n in range(terminal.shape[1] // width):
            cut = slice(n * width, (n + 1) * width)
            nodes = terminal[p : p + 1, cut]
            hot = jnp.concatenate(
                [hot_block(local, nodes, 2 * k + side) for k in range(count)], axis=0
            )
            both = dot(split[...], hot, NN)
            emit(p, cut, both[:scenarios] + both[scenarios:])


def gather_kernel(pos, terminal, volts, out, split):
    def emit(p, cut, value):
        out[p, :, cut] = value

    gather_into(pos[0], terminal, volts, split, emit)


def gather_rest(pos, terminal, volts, before, out, split):
    def emit(p, cut, value):
        out[p, :, cut] = before[p, :, cut] + value

    gather_into(1 - pos[0], terminal, volts, split, emit)


def scatter_into(side, terminal, split, emit):
    ends = split.shape[1]
    scenarios = split.shape[0] // 2
    local = block_places(ends)
    nodes = jnp.concatenate([terminal[p : p + 1, :] for p in range(3)], axis=1)
    for k in range(0, CHIPS, 2):
        hot = jnp.concatenate(
            [hot_block(local, nodes, 2 * (k + i) + side) for i in range(2)], axis=0
        )
        both = dot(split, hot, NT)
        value = both[:scenarios] + both[scenarios:]
        for i in range(2):
            emit(k + i, value[:, i * 128 : (i + 1) * 128])


def split_ends(h):
    parts = [stacked(h[p]) for p in range(3)]
    return jnp.concatenate(parts, axis=1)


def scatter_other(pos, terminal, h, out, split):
    def emit(k, value):
        out[k] = value

    split[...] = split_ends(h)
    scatter_into(1 - pos[0], terminal, split[...], emit)


def first_kernel(pos, terminal, volts, before, base, coef, term, h_out, out, split, ends):
    gather_rest(pos, terminal, volts, before, term, split)
    drop = mix(coef[0], term)
    for p in range(3):
        h_out[p] = base[p] - drop[p]
    scatter_other(pos, terminal, h_out, out, ends)


def scatter_mine(step, pos, terminal, h, source, drain, volts, out, split):
    def emit(k, value):
        out[k] = value

    split[...] = split_ends(h)
    scatter_into(pos[0], terminal, split[...], emit)
    me = pos[1]
    out[me] = out[me] + source[step] - drain[...] * volts[...]


def hot_places(places, count):
    owner = lax.broadcasted_iota(jnp.int32, (count, places.shape[1]), 0)
    return [ones_where(owner * 8 + r == places) for r in range(CAPACITY)]


def packed_lines(values):
    return -(-CAPACITY * values // 128)


def pack_kernel(pos, terminal, places, volts, before, surge2, h, term, packed, split):
    gather_rest(pos, terminal, volts, before, term, split)
    waves = [surge2[...] * term[p] - h[p] for p in range(3)]
    high, low = halves(jnp.concatenate(waves, axis=0))
    lines = packed_lines(high.shape[0])
    owners = packed.shape[0] // lines
    rows = []
    for hot in hot_places(places[...], owners):
        rows.append(dot(hot, high, NT) + dot(hot, low, NT))
    used = sum(r.shape[1] for r in rows)
    rows.append(jnp.zeros((owners, lines * 128 - used), F32))
    rows = jnp.concatenate(rows, axis=1)
    for k in range(lines):
        packed[pl.ds(k, owners, stride=lines), :] = rows[:, k * 128 : (k + 1) * 128]


def known_1(base, coef, t0, t1, out):
    a, b = mix(coef[1], t0), mix(coef[0], t1)
    for p in range(3):
        out[p] = base[p] - a[p] - b[p]


def known_2(base, coef, t0, t1, t2, a1, out):
    a, b, c = mix(coef[2], t0), mix(coef[1], t1), mix(coef[0], t2)
    d = mix(coef[STEPS + 1], a1)
    for p in range(3):
        out[p] = base[p] - a[p] - b[p] - c[p] + d[p]


def arrive_kernel(pos, terminal, places, packed, base, coef, arrived, h_out, out, ends):
    scenarios = base.shape[1]
    wide = 3 * scenarios
    lines = packed_lines(wide)
    owners = packed.shape[0] // lines
    rows = jnp.concatenate(
        [packed[pl.ds(k, owners, stride=lines), :] for k in range(lines)], axis=1
    )
    total = None
    for r, hot in enumerate(hot_places(places[...], owners)):
        high, low = halves(rows[:, r * wide : (r + 1) * wide])
        part = dot(high, hot, TN) + dot(low, hot, TN)
        total = part if total is None else total + part
    for p in range(3):
        arrived[p] = total[p * scenarios : (p + 1) * scenarios]
    gain = mix(coef[STEPS], arrived)
    for p in range(3):
        h_out[p] = base[p] + gain[p]
    scatter_other(pos, terminal, h_out, out, ends)


def last_kernel(pos, terminal, volts, before, surge, h, out, split):
    def emit(p, cut, value):
        term = before[p, :, cut] + value
        out[p, :, cut] = surge[:, cut] * term - h[p, :, cut]

    gather_into(1 - pos[0], terminal, volts, split, emit)


def total_kernel(parts, out):
    total = parts[0]
    for k in range(1, CHIPS):
        total = total + parts[k]
    for k in range(CHIPS):
        out[k] = total


def copies_kernel(a, b, rows, out):
    volts = a[...] + b[...]
    rows[...] = volts
    for k in range(CHIPS):
        out[k] = volts


def solve_kernel(current, inverse, out, split):
    count, scenarios, lanes = current.shape
    for k in range(count):
        high, low = halves(current[k])
        split[0:scenarios, k * lanes : (k + 1) * lanes] = high
        split[scenarios : 2 * scenarios, k * lanes : (k + 1) * lanes] = low
    both = dot(split[...], inverse[...], NT)
    out[...] = both[:scenarios, :lanes] + both[:scenarios, lanes:] + both[scenarios:, :lanes]


def exchanged(x):
    return lax.all_to_all(x, PLANE, 0, 0, tiled=True)


def swapped(x):
    return lax.ppermute(x, "core", [(0, 1), (1, 0)])


def on_device(
    conductance_inverse,
    prior_voltage,
    sources,
    fault_node,
    fault_conductance,
    terminal_node,
    ownership,
    partner,
    delay_steps,
    surge_conductance,
    pole_wave,
    residue_wave,
    pole_admit,
    residue_admit,
    wave_state,
    admit_state,
    wave_history,
):
    rows, node_count = conductance_inverse.shape[1:]
    scenarios = prior_voltage.shape[1]
    slots = ownership.shape[1]
    ends = 3 * slots
    devices = lax.axis_size(NET_LINE)
    net, z, y, core = (lax.axis_index(a) for a in NET_LINE)
    me = lax.axis_index(LINE)

    live = ownership[0] > 0
    live_float = live.astype(F32)[None]
    partners = partner[0]
    slot = jnp.arange(slots, dtype=jnp.int32)
    earlier = (
        (partners[:, None] == partners[None, :])
        & live[:, None]
        & (slot[:, None] < slot[None, :])
    )
    rank = jnp.sum(earlier.astype(jnp.int32), axis=0)
    places = jnp.where(live, partners * 8 + rank, -1)[None]
    terminal = terminal_node[0]
    surge = surge_conductance * live_float
    surge2 = 2.0 * surge
    lane = jnp.arange(rows, dtype=jnp.int32)[None]
    first_node = net * node_count + me * rows
    drain = jnp.where(
        fault_node[:, None] - first_node == lane, fault_conductance[:, None], 0.0
    )
    pos = jnp.stack([core, z * SIDE + y]).astype(jnp.int32)

    half = shape(CHIPS, scenarios, rows)
    waves = shape(3, scenarios, slots)
    splits = pltpu.VMEM((2 * scenarios, 16 * rows), BF16)
    end_split = pltpu.VMEM((2 * scenarios, ends), BF16)

    block = shape(scenarios, rows)

    def first_gather(plane):
        return call(gather_kernel, (pos,), (terminal, plane), waves, [splits], 4_000_000_000)

    def solve(h, other, step, voltage_rows):
        sent = swapped(other)
        mine = call(
            functools.partial(scatter_mine, step),
            (pos,),
            (terminal, h, sources, drain, voltage_rows),
            half,
            [end_split],
            4_000_000_000,
        )
        plane = exchanged(call(total_kernel, (), (exchanged(mine + sent),), half))
        other = call(solve_kernel, (), (plane, inverse_other), block, [splits], 500_000_000)
        sent = swapped(other)
        mine = call(solve_kernel, (), (plane, inverse_mine), block, [splits], 500_000_000)
        return call(copies_kernel, (), (mine, sent), (block, half))

    voltage_rows = prior_voltage[0]
    plane = exchanged(jnp.broadcast_to(voltage_rows[None], half.shape))
    small = (live_float, delay_steps, pole_wave[0], pole_admit[0])
    states = (wave_state[0], admit_state[0], wave_history[0])
    live_row, delays, poles_w, poles_a = small
    base_0, coef = fold(
        fold_first,
        (live_row, delays, poles_w, residue_wave[0], poles_a, residue_admit[0]),
        states,
        1,
        [shape(2 * STEPS + 2, 3, 3, slots)],
    )
    plane, base_0, coef = lax.optimization_barrier((plane, base_0, coef))
    base = [base_0, *fold(fold_later, (*small, coef), states, STEPS - 1, [])]
    inverse_mine, give = call(
        cut_kernel,
        (pos,),
        (conductance_inverse[0],),
        (shape(2 * rows, CHIPS * 128, dtype=BF16), shape(rows, CHIPS * 128)),
    )
    inverse_other = call(
        split_kernel, (), (swapped(give),), shape(2 * rows, CHIPS * 128, dtype=BF16)
    )
    far = swapped(plane)
    before = first_gather(plane)
    t0, h, other = call(
        first_kernel,
        (pos,),
        (terminal, far, before, base[0], coef),
        (waves, waves, half),
        [splits, end_split],
        8_000_000_000,
    )
    voltage_rows, copies = solve(h, other, 0, voltage_rows)
    terms = [t0]
    arrivals = []
    lines = packed_lines(3 * scenarios)
    packed_shape = shape(devices * lines, 128)
    for step in range(1, STEPS):
        plane = exchanged(copies)
        far = swapped(plane)
        before = first_gather(plane)
        term, packed = call(
            pack_kernel,
            (pos,),
            (terminal, places, far, before, surge2, h),
            (waves, packed_shape),
            [splits],
            5_000_000_000,
        )
        terms.append(term)
        packed = packed.reshape(devices, 1, lines * 128)
        packed = lax.all_to_all(packed, NET_LINE, 0, 0, tiled=True)
        packed = packed.reshape(devices * lines, 128)
        known = call((known_1, known_2)[step - 1], (), (base[step], coef, *terms, *arrivals), waves)
        arrived, h, other = call(
            arrive_kernel,
            (pos,),
            (terminal, places, packed, known, coef),
            (waves, waves, half),
            [end_split],
            5_000_000_000,
        )
        arrivals.append(arrived)
        voltage_rows, copies = solve(h, other, step, voltage_rows)
    plane = exchanged(copies)
    far = swapped(plane)
    before = first_gather(plane)
    current = call(
        last_kernel, (pos,), (terminal, far, before, surge, h), waves, [splits], 4_000_000_000
    )
    return voltage_rows[None], current[None]


def solution(mesh):
    finer = Mesh(mesh.devices.reshape(mesh.shape["net"], SIDE, SIDE, 2), NET_LINE)
    in_specs = (
        P("net", LINE, None),
        P("net", None, LINE),
        P(None, "net", LINE),
        P(),
        P(),
        P("net", None, LINE),
        P("net", LINE),
        P("net", LINE),
        P("net", LINE),
        P("net", LINE),
        P("net", None, LINE),
        P("net", None, None, None, LINE),
        P("net", None, LINE),
        P("net", None, None, None, LINE),
        P("net", None, None, None, LINE),
        P("net", None, None, None, LINE),
        P("net", None, None, None, LINE),
    )
    out_specs = (P("net", None, LINE), P("net", None, None, LINE))
    return jax.shard_map(
        on_device, mesh=finer, in_specs=in_specs, out_specs=out_specs, check_vma=False
    )
```

```python
import functools

import jax
import jax.numpy as jnp
from jax import lax
from jax.experimental import pallas as pl
from jax.experimental.pallas import tpu as pltpu
from jax.sharding import Mesh
from jax.sharding import PartitionSpec as P

STEPS = 3
PLANE = ("z", "y")
LINE = ("z", "y", "core")
NET_LINE = ("net", "z", "y", "core")
SIDE = 4
SURGE = 2 * STEPS + 2
CHIPS = SIDE * SIDE
CAPACITY = 5
F32 = jnp.float32
BF16 = jnp.bfloat16
VMEM = pl.BlockSpec(memory_space=pltpu.VMEM)
SMEM = pl.BlockSpec(memory_space=pltpu.SMEM)
PARAMS = pltpu.CompilerParams(vmem_limit_bytes=16 * 1024 * 1024)


def shape(*dims, dtype=F32):
    return jax.ShapeDtypeStruct(dims, dtype)


def estimate(arrays, outs, flops):
    moved = sum(a.size * a.dtype.itemsize for a in [*arrays, *jax.tree.leaves(outs)])
    return pl.CostEstimate(flops=flops, bytes_accessed=moved, transcendentals=0)


def call(kernel, scalars, arrays, outs, scratch=(), flops=1_000_000):
    return pl.pallas_call(
        kernel,
        out_shape=outs,
        in_specs=[SMEM] * len(scalars) + [VMEM] * len(arrays),
        out_specs=jax.tree.map(lambda _: VMEM, outs),
        scratch_shapes=list(scratch),
        compiler_params=PARAMS,
        cost_estimate=estimate(arrays, outs, flops),
    )(*scalars, *arrays)


def halves(x):
    high = x.astype(BF16)
    low = (x - high.astype(F32)).astype(BF16)
    return high, low


def stacked(x):
    return jnp.concatenate(halves(x), axis=0)


def ones_where(mask):
    return jnp.where(mask, 1.0, 0.0).astype(BF16)


def within_block(nodes, block):
    return jnp.clip(nodes - block * 128, -1, 128).astype(F32).astype(BF16)


def hot_block(local, nodes, block):
    one, zero = jnp.ones((), BF16), jnp.zeros((), BF16)
    return jnp.where(local == within_block(nodes, block), one, zero)


def block_places(width):
    return lax.broadcasted_iota(jnp.int32, (128, width), 0).astype(F32).astype(BF16)


def dot(a, b, dims):
    return lax.dot_general(a, b, (dims, ((), ())), preferred_element_type=F32)


def own_core():
    return lax.axis_index("core")


def own_chip():
    return lax.axis_index("z") * SIDE + lax.axis_index("y")


NN = ((1,), (0,))
NT = ((1,), (1,))
TN = ((0,), (0,))


def mix(coef, waves):
    return [
        coef[p, 0:1, :] * waves[0] + coef[p, 1:2, :] * waves[1] + coef[p, 2:3, :] * waves[2]
        for p in range(3)
    ]


def lag_coefficients(own, delay, surge, pw, rw, pa, ra, coef):
    live = own[...]
    steps = delay[...]
    coef[SURGE, 0, 0:1] = surge[...] * live
    coef[SURGE, 0, 1:2] = 2.0 * surge[...] * live
    coef[SURGE, 0, 2:3] = live
    for p in (1, 2):
        coef[SURGE, p] = jnp.zeros(coef.shape[2:], F32)
    first = (steps == 1).astype(F32)
    second = (steps == 2).astype(F32)
    for p in range(3):
        lags = []
        for pole, res in ((pa, ra), (pw, rw)):
            terms = [res[q, p] for q in range(pole.shape[0])]
            for m in range(STEPS):
                if m:
                    terms = [x * pole[q : q + 1, :] for q, x in enumerate(terms)]
                lags.append(sum(terms[1:], terms[0]) * live)
        for m in range(STEPS):
            coef[m, p] = lags[m]
            coef[STEPS + 2 + m, p] = lags[STEPS + m]
        coef[STEPS, p] = lags[STEPS] * first
        coef[STEPS + 1, p] = lags[STEPS + 1] * first + lags[STEPS] * second


def fold_states(times, own, delay, pw, pa, coef, xw, xa, hist, outs):
    live = own[...]
    steps = delay[...]
    delayed = []
    for age in range(max(times) + 1):
        rows = []
        for r in range(3):
            w = None
            for k in range(hist.shape[0] - age):
                part = jnp.where(steps == k + 1 + age, hist[k, r], 0.0)
                w = part if w is None else w + part
            rows.append(w)
        delayed.append(rows)
    for p in range(3):
        totals = {}
        for q in range(pw.shape[0]):
            w_now = xw[q, p]
            a_now = xa[q, p]
            for t in range(max(times) + 1):
                w_now = w_now * pw[q : q + 1, :]
                a_now = a_now * pa[q : q + 1, :]
                if t in times:
                    part = w_now - a_now
                    totals[t] = totals[t] + part if t in totals else part
        for t, out in zip(times, outs):
            value = totals[t] * live
            for s in range(t + 1):
                lag = STEPS + 2 + t - s
                for r in range(3):
                    value = value + coef[lag, p, r : r + 1, :] * delayed[s][r]
            out[p] = value


def fold_first(own, delay, surge, pw, rw, pa, ra, xw, xa, hist, out, coef):
    @pl.when(pl.program_id(0) == 0)
    def _():
        lag_coefficients(own, delay, surge, pw, rw, pa, ra, coef)

    fold_states((0,), own, delay, pw, pa, coef, xw, xa, hist, (out,))


def fold_later(own, delay, pw, pa, coef, xw, xa, hist, *outs):
    fold_states((1, 2), own, delay, pw, pa, coef, xw, xa, hist, outs)


def fold(kernel, small, states, bases, coefs):
    poles, _, scenarios, slots = states[0].shape
    tile = 16
    whole = lambda a: pl.BlockSpec(a.shape, lambda i: (0,) * len(a.shape))
    cut = lambda a: pl.BlockSpec((*a.shape[:2], tile, slots), lambda i: (0, 0, i, 0))
    out = shape(3, scenarios, slots)
    outs = [out] * bases + coefs
    return pl.pallas_call(
        kernel,
        grid=(scenarios // tile,),
        out_shape=outs,
        in_specs=[whole(a) for a in small] + [cut(a) for a in states],
        out_specs=[pl.BlockSpec((3, tile, slots), lambda i: (0, i, 0))] * bases
        + [whole(a) for a in coefs],
        compiler_params=PARAMS,
        cost_estimate=estimate((*small, *states), outs, 20_000_000),
    )(*small, *states)


def cut_kernel(inverse, mine, give):
    rows = inverse.shape[0]
    for k in range(CHIPS):
        lanes = slice(k * 128, (k + 1) * 128)
        start = pl.multiple_of((k * 2 + own_core()) * 128, 128)
        high, low = halves(inverse[:, pl.ds(start, 128)])
        mine[0:rows, lanes] = high
        mine[rows : 2 * rows, lanes] = low
        start = pl.multiple_of((k * 2 + 1 - own_core()) * 128, 128)
        give[:, lanes] = inverse[:, pl.ds(start, 128)]


def split_kernel(inverse, out):
    rows = inverse.shape[0]
    high, low = halves(inverse[...])
    out[0:rows] = high
    out[rows : 2 * rows] = low


def gather_into(side, terminal, volts, split, emit):
    count, scenarios, lanes = volts.shape
    for k in range(count):
        high, low = halves(volts[k])
        split[0:scenarios, k * lanes : (k + 1) * lanes] = high
        split[scenarios : 2 * scenarios, k * lanes : (k + 1) * lanes] = low
    width = 256
    local = block_places(width)
    for p in range(3):
        for n in range(terminal.shape[1] // width):
            cut = slice(n * width, (n + 1) * width)
            nodes = terminal[p : p + 1, cut]
            hot = jnp.concatenate(
                [hot_block(local, nodes, 2 * k + side) for k in range(count)], axis=0
            )
            both = dot(split[...], hot, NN)
            emit(p, cut, both[:scenarios] + both[scenarios:])


def gather_kernel(terminal, volts, out, split):
    def emit(p, cut, value):
        out[p, :, cut] = value

    gather_into(own_core(), terminal, volts, split, emit)


def gather_rest(terminal, volts, before, out, split):
    def emit(p, cut, value):
        out[p, :, cut] = before[p, :, cut] + value

    gather_into(1 - own_core(), terminal, volts, split, emit)


def scatter_into(side, terminal, split, emit):
    ends = split.shape[1]
    scenarios = split.shape[0] // 2
    local = block_places(ends)
    nodes = jnp.concatenate([terminal[p : p + 1, :] for p in range(3)], axis=1)
    for k in range(0, CHIPS, 2):
        hot = jnp.concatenate(
            [hot_block(local, nodes, 2 * (k + i) + side) for i in range(2)], axis=0
        )
        both = dot(split, hot, NT)
        value = both[:scenarios] + both[scenarios:]
        for i in range(2):
            emit(k + i, value[:, i * 128 : (i + 1) * 128])


def split_ends(h):
    parts = [stacked(h[p]) for p in range(3)]
    return jnp.concatenate(parts, axis=1)


def scatter_other(terminal, h, ends, out):
    def emit(k, value):
        out[k] = value

    ends[...] = split_ends(h)
    scatter_into(1 - own_core(), terminal, ends[...], emit)


def first_kernel(terminal, volts, before, base, coef, term, h_out, ends, out, split):
    gather_rest(terminal, volts, before, term, split)
    drop = mix(coef[0], term)
    for p in range(3):
        h_out[p] = base[p] - drop[p]
    scatter_other(terminal, h_out, ends, out)


def scatter_mine(step, terminal, ends, source, drain, volts, out):
    def emit(k, value):
        out[k] = value

    scatter_into(own_core(), terminal, ends[...], emit)
    me = own_chip()
    out[me] = out[me] + source[step] - drain[...] * volts[...]


def hot_places(places, count):
    owner = lax.broadcasted_iota(jnp.int32, (count, places.shape[1]), 0)
    return [ones_where(owner * 8 + r == places) for r in range(CAPACITY)]


def packed_lines(values):
    return -(-CAPACITY * values // 128)


def pack_kernel(terminal, volts, before, coef, h, term, packed, split):
    gather_rest(terminal, volts, before, term, split)
    surge2 = coef[SURGE, 0, 1:2, :]
    waves = [surge2 * term[p] - h[p] for p in range(3)]
    high, low = halves(jnp.concatenate(waves, axis=0))
    lines = packed_lines(high.shape[0])
    owners = packed.shape[0] // lines
    rows = []
    for hot in hot_places(terminal[3:4, :], owners):
        rows.append(dot(hot, high, NT) + dot(hot, low, NT))
    used = sum(r.shape[1] for r in rows)
    rows.append(jnp.zeros((owners, lines * 128 - used), F32))
    rows = jnp.concatenate(rows, axis=1)
    for k in range(lines):
        packed[pl.ds(k, owners, stride=lines), :] = rows[:, k * 128 : (k + 1) * 128]


def known_1(base, coef, t0, t1, out):
    a, b = mix(coef[1], t0), mix(coef[0], t1)
    for p in range(3):
        out[p] = base[p] - a[p] - b[p]


def known_2(base, coef, t0, t1, t2, a1, out):
    a, b, c = mix(coef[2], t0), mix(coef[1], t1), mix(coef[0], t2)
    d = mix(coef[STEPS + 1], a1)
    for p in range(3):
        out[p] = base[p] - a[p] - b[p] - c[p] + d[p]


def arrive_kernel(terminal, packed, base, coef, arrived, h_out, ends, out):
    scenarios = base.shape[1]
    wide = 3 * scenarios
    lines = packed_lines(wide)
    owners = packed.shape[0] // lines
    rows = jnp.concatenate(
        [packed[pl.ds(k, owners, stride=lines), :] for k in range(lines)], axis=1
    )
    total = None
    for r, hot in enumerate(hot_places(terminal[3:4, :], owners)):
        high, low = halves(rows[:, r * wide : (r + 1) * wide])
        part = dot(high, hot, TN) + dot(low, hot, TN)
        total = part if total is None else total + part
    for p in range(3):
        arrived[p] = total[p * scenarios : (p + 1) * scenarios]
    gain = mix(coef[STEPS], arrived)
    for p in range(3):
        h_out[p] = base[p] + gain[p]
    scatter_other(terminal, h_out, ends, out)


def last_kernel(terminal, volts, before, coef, h, out, split):
    surge = coef[SURGE, 0, 0:1, :]

    def emit(p, cut, value):
        term = before[p, :, cut] + value
        out[p, :, cut] = surge[:, cut] * term - h[p, :, cut]

    gather_into(1 - own_core(), terminal, volts, split, emit)


def total_kernel(parts, out):
    total = parts[0]
    for k in range(1, CHIPS):
        total = total + parts[k]
    for k in range(CHIPS):
        out[k] = total


def copies_kernel(a, b, rows, out):
    volts = a[...] + b[...]
    rows[...] = volts
    for k in range(CHIPS):
        out[k] = volts


def solve_kernel(current, inverse, out, split):
    count, scenarios, lanes = current.shape
    for k in range(count):
        high, low = halves(current[k])
        split[0:scenarios, k * lanes : (k + 1) * lanes] = high
        split[scenarios : 2 * scenarios, k * lanes : (k + 1) * lanes] = low
    both = dot(split[...], inverse[...], NT)
    out[...] = both[:scenarios, :lanes] + both[:scenarios, lanes:] + both[scenarios:, :lanes]


def exchanged(x):
    return lax.all_to_all(x, PLANE, 0, 0, tiled=True)


def swapped(x):
    return lax.ppermute(x, "core", [(0, 1), (1, 0)])


def on_device(
    conductance_inverse,
    prior_voltage,
    sources,
    fault_node,
    fault_conductance,
    terminal_node,
    ownership,
    partner,
    delay_steps,
    surge_conductance,
    pole_wave,
    residue_wave,
    pole_admit,
    residue_admit,
    wave_state,
    admit_state,
    wave_history,
):
    rows, node_count = conductance_inverse.shape[1:]
    scenarios = prior_voltage.shape[1]
    slots = ownership.shape[1]
    ends = 3 * slots
    devices = lax.axis_size(NET_LINE)
    net, z, y, core = (lax.axis_index(a) for a in NET_LINE)
    me = lax.axis_index(LINE)

    live = ownership[0] > 0
    live_float = live.astype(F32)[None]
    partners = partner[0]
    slot = jnp.arange(slots, dtype=jnp.int32)
    earlier = (
        (partners[:, None] == partners[None, :])
        & live[:, None]
        & (slot[:, None] < slot[None, :])
    )
    rank = jnp.sum(earlier.astype(jnp.int32), axis=0)
    places = jnp.where(live, partners * 8 + rank, -1)[None]
    table = jnp.concatenate([terminal_node[0], places], axis=0)
    lane = jnp.arange(rows, dtype=jnp.int32)[None]
    first_node = net * node_count + me * rows
    drain = jnp.where(
        fault_node[:, None] - first_node == lane, fault_conductance[:, None], 0.0
    )

    half = shape(CHIPS, scenarios, rows)
    waves = shape(3, scenarios, slots)
    splits = pltpu.VMEM((2 * scenarios, 16 * rows), BF16)
    end_split = shape(2 * scenarios, ends, dtype=BF16)

    block = shape(scenarios, rows)

    def first_gather(plane):
        return call(gather_kernel, (), (table, plane), waves, [splits], 4_000_000_000)

    def solve(ends_split, other, step, voltage_rows):
        sent = swapped(other)
        mine = call(
            functools.partial(scatter_mine, step),
            (),
            (table, ends_split, sources, drain, voltage_rows),
            half,
            (),
            4_000_000_000,
        )
        plane = exchanged(call(total_kernel, (), (exchanged(mine + sent),), half))
        other = call(solve_kernel, (), (plane, inverse_other), block, [splits], 500_000_000)
        sent = swapped(other)
        mine = call(solve_kernel, (), (plane, inverse_mine), block, [splits], 500_000_000)
        return call(copies_kernel, (), (mine, sent), (block, half))

    voltage_rows = prior_voltage[0]
    plane = exchanged(jnp.broadcast_to(voltage_rows[None], half.shape))
    small = (live_float, delay_steps, pole_wave[0], pole_admit[0])
    states = (wave_state[0], admit_state[0], wave_history[0])
    live_row, delays, poles_w, poles_a = small
    base_0, coef = fold(
        fold_first,
        (
            live_row,
            delays,
            surge_conductance,
            poles_w,
            residue_wave[0],
            poles_a,
            residue_admit[0],
        ),
        states,
        1,
        [shape(SURGE + 1, 3, 3, slots)],
    )
    plane, base_0, coef, table = lax.optimization_barrier((plane, base_0, coef, table))
    base = [base_0, *fold(fold_later, (*small, coef), states, STEPS - 1, [])]
    inverse_mine, give = call(
        cut_kernel,
        (),
        (conductance_inverse[0],),
        (shape(2 * rows, CHIPS * 128, dtype=BF16), shape(rows, CHIPS * 128)),
    )
    inverse_other = call(
        split_kernel, (), (swapped(give),), shape(2 * rows, CHIPS * 128, dtype=BF16)
    )
    far = swapped(plane)
    before = first_gather(plane)
    t0, h, ends_split, other = call(
        first_kernel,
        (),
        (table, far, before, base[0], coef),
        (waves, waves, end_split, half),
        [splits],
        8_000_000_000,
    )
    voltage_rows, copies = solve(ends_split, other, 0, voltage_rows)
    terms = [t0]
    arrivals = []
    lines = packed_lines(3 * scenarios)
    packed_shape = shape(devices * lines, 128)
    for step in range(1, STEPS):
        plane = exchanged(copies)
        far = swapped(plane)
        before = first_gather(plane)
        term, packed = call(
            pack_kernel,
            (),
            (table, far, before, coef, h),
            (waves, packed_shape),
            [splits],
            5_000_000_000,
        )
        terms.append(term)
        packed = packed.reshape(devices, 1, lines * 128)
        packed = lax.all_to_all(packed, NET_LINE, 0, 0, tiled=True)
        packed = packed.reshape(devices * lines, 128)
        known = call((known_1, known_2)[step - 1], (), (base[step], coef, *terms, *arrivals), waves)
        arrived, h, ends_split, other = call(
            arrive_kernel,
            (),
            (table, packed, known, coef),
            (waves, waves, end_split, half),
            (),
            5_000_000_000,
        )
        arrivals.append(arrived)
        voltage_rows, copies = solve(ends_split, other, step, voltage_rows)
    plane = exchanged(copies)
    far = swapped(plane)
    before = first_gather(plane)
    current = call(
        last_kernel, (), (table, far, before, coef, h), waves, [splits], 4_000_000_000
    )
    return voltage_rows[None], current[None]


def solution(mesh):
    finer = Mesh(mesh.devices.reshape(mesh.shape["net"], SIDE, SIDE, 2), NET_LINE)
    in_specs = (
        P("net", LINE, None),
        P("net", None, LINE),
        P(None, "net", LINE),
        P(),
        P(),
        P("net", None, LINE),
        P("net", LINE),
        P("net", LINE),
        P("net", LINE),
        P("net", LINE),
        P("net", None, LINE),
        P("net", None, None, None, LINE),
        P("net", None, LINE),
        P("net", None, None, None, LINE),
        P("net", None, None, None, LINE),
        P("net", None, None, None, LINE),
        P("net", None, None, None, LINE),
    )
    out_specs = (P("net", None, LINE), P("net", None, None, LINE))
    return jax.shard_map(
        on_device, mesh=finer, in_specs=in_specs, out_specs=out_specs, check_vma=False
    )
```

```python
import functools

import jax
import jax.numpy as jnp
from jax import lax
from jax.experimental import pallas as pl
from jax.experimental.pallas import tpu as pltpu
from jax.sharding import Mesh
from jax.sharding import PartitionSpec as P

STEPS = 3
PLANE = ("z", "y")
LINE = ("z", "y", "core")
NET_LINE = ("net", "z", "y", "core")
SIDE = 4
SURGE = 2 * STEPS + 2
CHIPS = SIDE * SIDE
CAPACITY = 5
F32 = jnp.float32
BF16 = jnp.bfloat16
VMEM = pl.BlockSpec(memory_space=pltpu.VMEM)
SMEM = pl.BlockSpec(memory_space=pltpu.SMEM)
PARAMS = pltpu.CompilerParams(vmem_limit_bytes=16 * 1024 * 1024)


def shape(*dims, dtype=F32):
    return jax.ShapeDtypeStruct(dims, dtype)


def estimate(arrays, outs, flops):
    moved = sum(a.size * a.dtype.itemsize for a in [*arrays, *jax.tree.leaves(outs)])
    return pl.CostEstimate(flops=flops, bytes_accessed=moved, transcendentals=0)


def call(kernel, scalars, arrays, outs, scratch=(), flops=1_000_000):
    return pl.pallas_call(
        kernel,
        out_shape=outs,
        in_specs=[SMEM] * len(scalars) + [VMEM] * len(arrays),
        out_specs=jax.tree.map(lambda _: VMEM, outs),
        scratch_shapes=list(scratch),
        compiler_params=PARAMS,
        cost_estimate=estimate(arrays, outs, flops),
    )(*scalars, *arrays)


def halves(x):
    high = x.astype(BF16)
    low = (x - high.astype(F32)).astype(BF16)
    return high, low


def stacked(x):
    return jnp.concatenate(halves(x), axis=0)


def ones_where(mask):
    return jnp.where(mask, 1.0, 0.0).astype(BF16)


def within_block(nodes, block):
    return jnp.clip(nodes - block * 128, -1, 128).astype(F32).astype(BF16)


def hot_block(local, nodes, block):
    one, zero = jnp.ones((), BF16), jnp.zeros((), BF16)
    return jnp.where(local == within_block(nodes, block), one, zero)


def block_places(width):
    return lax.broadcasted_iota(jnp.int32, (128, width), 0).astype(F32).astype(BF16)


def dot(a, b, dims):
    return lax.dot_general(a, b, (dims, ((), ())), preferred_element_type=F32)


def own_core():
    return lax.axis_index("core")


def own_chip():
    return lax.axis_index("z") * SIDE + lax.axis_index("y")


NN = ((1,), (0,))
NT = ((1,), (1,))
TN = ((0,), (0,))


def mix(coef, waves):
    return [
        coef[p, 0:1, :] * waves[0] + coef[p, 1:2, :] * waves[1] + coef[p, 2:3, :] * waves[2]
        for p in range(3)
    ]


def lag_coefficients(own, delay, surge, pw, rw, pa, ra, coef):
    live = own[...]
    steps = delay[...]
    coef[SURGE, 0, 0:1] = surge[...] * live
    coef[SURGE, 0, 1:2] = 2.0 * surge[...] * live
    coef[SURGE, 0, 2:3] = live
    for p in (1, 2):
        coef[SURGE, p] = jnp.zeros(coef.shape[2:], F32)
    first = (steps == 1).astype(F32)
    second = (steps == 2).astype(F32)
    for p in range(3):
        lags = []
        for pole, res in ((pa, ra), (pw, rw)):
            terms = [res[q, p] for q in range(pole.shape[0])]
            for m in range(STEPS):
                if m:
                    terms = [x * pole[q : q + 1, :] for q, x in enumerate(terms)]
                lags.append(sum(terms[1:], terms[0]) * live)
        for m in range(STEPS):
            coef[m, p] = lags[m]
            coef[STEPS + 2 + m, p] = lags[STEPS + m]
        coef[STEPS, p] = lags[STEPS] * first
        coef[STEPS + 1, p] = lags[STEPS + 1] * first + lags[STEPS] * second


def fold_states(times, own, delay, pw, pa, coef, xw, xa, hist, outs):
    live = own[...]
    steps = delay[...]
    delayed = []
    for age in range(max(times) + 1):
        rows = []
        for r in range(3):
            w = None
            for k in range(hist.shape[0] - age):
                part = jnp.where(steps == k + 1 + age, hist[k, r], 0.0)
                w = part if w is None else w + part
            rows.append(w)
        delayed.append(rows)
    for p in range(3):
        totals = {}
        for q in range(pw.shape[0]):
            w_now = xw[q, p]
            a_now = xa[q, p]
            for t in range(max(times) + 1):
                w_now = w_now * pw[q : q + 1, :]
                a_now = a_now * pa[q : q + 1, :]
                if t in times:
                    part = w_now - a_now
                    totals[t] = totals[t] + part if t in totals else part
        for t, out in zip(times, outs):
            value = totals[t] * live
            for s in range(t + 1):
                lag = STEPS + 2 + t - s
                for r in range(3):
                    value = value + coef[lag, p, r : r + 1, :] * delayed[s][r]
            out[p] = value


def fold_first(own, delay, surge, pw, rw, pa, ra, xw, xa, hist, out, coef):
    @pl.when(pl.program_id(0) == 0)
    def _():
        lag_coefficients(own, delay, surge, pw, rw, pa, ra, coef)

    fold_states((0,), own, delay, pw, pa, coef, xw, xa, hist, (out,))


def fold_later(own, delay, pw, pa, coef, xw, xa, hist, *outs):
    fold_states((1, 2), own, delay, pw, pa, coef, xw, xa, hist, outs)


def fold(kernel, small, states, bases, coefs):
    poles, _, scenarios, slots = states[0].shape
    tile = 16
    whole = lambda a: pl.BlockSpec(a.shape, lambda i: (0,) * len(a.shape))
    cut = lambda a: pl.BlockSpec((*a.shape[:2], tile, slots), lambda i: (0, 0, i, 0))
    out = shape(3, scenarios, slots)
    outs = [out] * bases + coefs
    return pl.pallas_call(
        kernel,
        grid=(scenarios // tile,),
        out_shape=outs,
        in_specs=[whole(a) for a in small] + [cut(a) for a in states],
        out_specs=[pl.BlockSpec((3, tile, slots), lambda i: (0, i, 0))] * bases
        + [whole(a) for a in coefs],
        compiler_params=PARAMS,
        cost_estimate=estimate((*small, *states), outs, 20_000_000),
    )(*small, *states)


def cut_kernel(inverse, mine, give):
    rows = inverse.shape[0]
    for k in range(CHIPS):
        lanes = slice(k * 128, (k + 1) * 128)
        start = pl.multiple_of((k * 2 + own_core()) * 128, 128)
        high, low = halves(inverse[:, pl.ds(start, 128)])
        mine[0:rows, lanes] = high
        mine[rows : 2 * rows, lanes] = low
        start = pl.multiple_of((k * 2 + 1 - own_core()) * 128, 128)
        give[:, lanes] = inverse[:, pl.ds(start, 128)]


def split_kernel(inverse, out):
    rows = inverse.shape[0]
    high, low = halves(inverse[...])
    out[0:rows] = high
    out[rows : 2 * rows] = low


def gather_into(side, terminal, volts, split, emit):
    count, scenarios, lanes = volts.shape
    for k in range(count):
        high, low = halves(volts[k])
        split[0:scenarios, k * lanes : (k + 1) * lanes] = high
        split[scenarios : 2 * scenarios, k * lanes : (k + 1) * lanes] = low
    width = 256
    local = block_places(width)
    for p in range(3):
        for n in range(terminal.shape[1] // width):
            cut = slice(n * width, (n + 1) * width)
            nodes = terminal[p : p + 1, cut]
            hot = jnp.concatenate(
                [hot_block(local, nodes, 2 * k + side) for k in range(count)], axis=0
            )
            both = dot(split[...], hot, NN)
            emit(p, cut, both[:scenarios] + both[scenarios:])


def gather_kernel(terminal, volts, out, split):
    def emit(p, cut, value):
        out[p, :, cut] = value

    gather_into(own_core(), terminal, volts, split, emit)


def gather_rest(terminal, volts, before, out, split):
    def emit(p, cut, value):
        out[p, :, cut] = before[p, :, cut] + value

    gather_into(1 - own_core(), terminal, volts, split, emit)


def scatter_into(side, terminal, split, emit):
    ends = split.shape[1]
    scenarios = split.shape[0] // 2
    local = block_places(ends)
    nodes = jnp.concatenate([terminal[p : p + 1, :] for p in range(3)], axis=1)
    for k in range(0, CHIPS, 2):
        hot = jnp.concatenate(
            [hot_block(local, nodes, 2 * (k + i) + side) for i in range(2)], axis=0
        )
        both = dot(split, hot, NT)
        value = both[:scenarios] + both[scenarios:]
        for i in range(2):
            emit(k + i, value[:, i * 128 : (i + 1) * 128])


def split_ends(h):
    parts = [stacked(h[p]) for p in range(3)]
    return jnp.concatenate(parts, axis=1)


def scatter_other(terminal, h, ends, out):
    def emit(k, value):
        out[k] = value

    ends[...] = split_ends(h)
    scatter_into(1 - own_core(), terminal, ends[...], emit)


def first_kernel(terminal, volts, before, base, coef, term, h_out, ends, out, split):
    gather_rest(terminal, volts, before, term, split)
    drop = mix(coef[0], term)
    for p in range(3):
        h_out[p] = base[p] - drop[p]
    scatter_other(terminal, h_out, ends, out)


def scatter_mine(step, terminal, ends, source, drain, volts, out):
    def emit(k, value):
        out[k] = value

    scatter_into(own_core(), terminal, ends[...], emit)
    me = own_chip()
    out[me] = out[me] + source[step] - drain[...] * volts[...]


def hot_places(places, count):
    owner = lax.broadcasted_iota(jnp.int32, (count, places.shape[1]), 0)
    return [ones_where(owner * 8 + r == places) for r in range(CAPACITY)]


def packed_lines(values):
    return -(-CAPACITY * values // 128)


def pack_kernel(terminal, volts, before, coef, h, base, *refs):
    *past, term, packed, known, split = refs
    gather_rest(terminal, volts, before, term, split)
    surge2 = coef[SURGE, 0, 1:2, :]
    waves = [surge2 * term[p] - h[p] for p in range(3)]
    high, low = halves(jnp.concatenate(waves, axis=0))
    if len(past) == 1:
        drops = [mix(coef[1], past[0]), mix(coef[0], term)]
        gains = []
    else:
        drops = [mix(coef[2], past[0]), mix(coef[1], past[1]), mix(coef[0], term)]
        gains = [mix(coef[STEPS + 1], past[2])]
    for p in range(3):
        value = base[p]
        for drop in drops:
            value = value - drop[p]
        for gain in gains:
            value = value + gain[p]
        known[p] = value
    lines = packed_lines(high.shape[0])
    owners = packed.shape[0] // lines
    rows = []
    for hot in hot_places(terminal[3:4, :], owners):
        rows.append(dot(hot, high, NT) + dot(hot, low, NT))
    used = sum(r.shape[1] for r in rows)
    rows.append(jnp.zeros((owners, lines * 128 - used), F32))
    rows = jnp.concatenate(rows, axis=1)
    for k in range(lines):
        packed[pl.ds(k, owners, stride=lines), :] = rows[:, k * 128 : (k + 1) * 128]


def arrive_kernel(terminal, packed, base, coef, arrived, h_out, ends, out):
    scenarios = base.shape[1]
    wide = 3 * scenarios
    lines = packed_lines(wide)
    owners = packed.shape[0] // lines
    rows = jnp.concatenate(
        [packed[pl.ds(k, owners, stride=lines), :] for k in range(lines)], axis=1
    )
    total = None
    for r, hot in enumerate(hot_places(terminal[3:4, :], owners)):
        high, low = halves(rows[:, r * wide : (r + 1) * wide])
        part = dot(high, hot, TN) + dot(low, hot, TN)
        total = part if total is None else total + part
    for p in range(3):
        arrived[p] = total[p * scenarios : (p + 1) * scenarios]
    gain = mix(coef[STEPS], arrived)
    for p in range(3):
        h_out[p] = base[p] + gain[p]
    scatter_other(terminal, h_out, ends, out)


def last_kernel(terminal, volts, before, coef, h, out, split):
    surge = coef[SURGE, 0, 0:1, :]

    def emit(p, cut, value):
        term = before[p, :, cut] + value
        out[p, :, cut] = surge[:, cut] * term - h[p, :, cut]

    gather_into(1 - own_core(), terminal, volts, split, emit)


def total_kernel(parts, out):
    total = parts[0]
    for k in range(1, CHIPS):
        total = total + parts[k]
    for k in range(CHIPS):
        out[k] = total


def copies_kernel(a, b, rows, out):
    volts = a[...] + b[...]
    rows[...] = volts
    for k in range(CHIPS):
        out[k] = volts


def solve_kernel(current, inverse, out, split):
    count, scenarios, lanes = current.shape
    for k in range(count):
        high, low = halves(current[k])
        split[0:scenarios, k * lanes : (k + 1) * lanes] = high
        split[scenarios : 2 * scenarios, k * lanes : (k + 1) * lanes] = low
    both = dot(split[...], inverse[...], NT)
    out[...] = both[:scenarios, :lanes] + both[:scenarios, lanes:] + both[scenarios:, :lanes]


def exchanged(x):
    return lax.all_to_all(x, PLANE, 0, 0, tiled=True)


def swapped(x):
    return lax.ppermute(x, "core", [(0, 1), (1, 0)])


def on_device(
    conductance_inverse,
    prior_voltage,
    sources,
    fault_node,
    fault_conductance,
    terminal_node,
    ownership,
    partner,
    delay_steps,
    surge_conductance,
    pole_wave,
    residue_wave,
    pole_admit,
    residue_admit,
    wave_state,
    admit_state,
    wave_history,
):
    rows, node_count = conductance_inverse.shape[1:]
    scenarios = prior_voltage.shape[1]
    slots = ownership.shape[1]
    ends = 3 * slots
    devices = lax.axis_size(NET_LINE)
    net, z, y, core = (lax.axis_index(a) for a in NET_LINE)
    me = lax.axis_index(LINE)

    live = ownership[0] > 0
    live_float = live.astype(F32)[None]
    partners = partner[0]
    slot = jnp.arange(slots, dtype=jnp.int32)
    earlier = (
        (partners[:, None] == partners[None, :])
        & live[:, None]
        & (slot[:, None] < slot[None, :])
    )
    rank = jnp.sum(earlier.astype(jnp.int32), axis=0)
    places = jnp.where(live, partners * 8 + rank, -1)[None]
    table = jnp.concatenate([terminal_node[0], places], axis=0)
    lane = jnp.arange(rows, dtype=jnp.int32)[None]
    first_node = net * node_count + me * rows
    drain = jnp.where(
        fault_node[:, None] - first_node == lane, fault_conductance[:, None], 0.0
    )

    half = shape(CHIPS, scenarios, rows)
    waves = shape(3, scenarios, slots)
    splits = pltpu.VMEM((2 * scenarios, 16 * rows), BF16)
    end_split = shape(2 * scenarios, ends, dtype=BF16)

    block = shape(scenarios, rows)

    def first_gather(plane):
        return call(gather_kernel, (), (table, plane), waves, [splits], 4_000_000_000)

    def finish_constants(states, coef, inverse):
        later = fold(fold_later, (*small, coef), states, STEPS - 1, [])
        mine, give = call(
            cut_kernel,
            (),
            (inverse,),
            (shape(2 * rows, CHIPS * 128, dtype=BF16), shape(rows, CHIPS * 128)),
        )
        other = call(
            split_kernel, (), (swapped(give),), shape(2 * rows, CHIPS * 128, dtype=BF16)
        )
        return later, mine, other

    def reduce(ends_split, other, step, voltage_rows):
        sent = swapped(other)
        mine = call(
            functools.partial(scatter_mine, step),
            (),
            (table, ends_split, sources, drain, voltage_rows),
            half,
            (),
            4_000_000_000,
        )
        return mine + sent

    def solve(currents, inverse_mine, inverse_other):
        plane = exchanged(call(total_kernel, (), (currents,), half))
        other = call(solve_kernel, (), (plane, inverse_other), block, [splits], 500_000_000)
        sent = swapped(other)
        mine = call(solve_kernel, (), (plane, inverse_mine), block, [splits], 500_000_000)
        return call(copies_kernel, (), (mine, sent), (block, half))

    voltage_rows = prior_voltage[0]
    plane = exchanged(jnp.broadcast_to(voltage_rows[None], half.shape))
    small = (live_float, delay_steps, pole_wave[0], pole_admit[0])
    states = (wave_state[0], admit_state[0], wave_history[0])
    live_row, delays, poles_w, poles_a = small
    base_0, coef = fold(
        fold_first,
        (
            live_row,
            delays,
            surge_conductance,
            poles_w,
            residue_wave[0],
            poles_a,
            residue_admit[0],
        ),
        states,
        1,
        [shape(SURGE + 1, 3, 3, slots)],
    )
    plane, base_0, coef, table = lax.optimization_barrier((plane, base_0, coef, table))
    far = swapped(plane)
    before = first_gather(plane)
    t0, h, ends_split, other = call(
        first_kernel,
        (),
        (table, far, before, base_0, coef),
        (waves, waves, end_split, half),
        [splits],
        8_000_000_000,
    )
    currents, *inputs = lax.optimization_barrier(
        (reduce(ends_split, other, 0, voltage_rows), states, coef, conductance_inverse[0])
    )
    constants = finish_constants(*inputs)
    currents = exchanged(currents)
    currents, constants = lax.optimization_barrier((currents, constants))
    later, *inverses = constants
    base = [base_0, *later]
    voltage_rows, copies = solve(currents, *inverses)
    terms = [t0]
    arrivals = []
    lines = packed_lines(3 * scenarios)
    packed_shape = shape(devices * lines, 128)
    for step in range(1, STEPS):
        plane = exchanged(copies)
        far = swapped(plane)
        before = first_gather(plane)
        term, packed, known = call(
            pack_kernel,
            (),
            (table, far, before, coef, h, base[step], *terms, *arrivals),
            (waves, packed_shape, waves),
            [splits],
            5_000_000_000,
        )
        terms.append(term)
        packed = packed.reshape(devices, 1, lines * 128)
        packed = lax.all_to_all(packed, NET_LINE, 0, 0, tiled=True)
        packed = packed.reshape(devices * lines, 128)
        arrived, h, ends_split, other = call(
            arrive_kernel,
            (),
            (table, packed, known, coef),
            (waves, waves, end_split, half),
            (),
            5_000_000_000,
        )
        arrivals.append(arrived)
        currents = exchanged(reduce(ends_split, other, step, voltage_rows))
        voltage_rows, copies = solve(currents, *inverses)
    plane = exchanged(copies)
    far = swapped(plane)
    before = first_gather(plane)
    current = call(
        last_kernel, (), (table, far, before, coef, h), waves, [splits], 4_000_000_000
    )
    return voltage_rows[None], current[None]


def solution(mesh):
    finer = Mesh(mesh.devices.reshape(mesh.shape["net"], SIDE, SIDE, 2), NET_LINE)
    in_specs = (
        P("net", LINE, None),
        P("net", None, LINE),
        P(None, "net", LINE),
        P(),
        P(),
        P("net", None, LINE),
        P("net", LINE),
        P("net", LINE),
        P("net", LINE),
        P("net", LINE),
        P("net", None, LINE),
        P("net", None, None, None, LINE),
        P("net", None, LINE),
        P("net", None, None, None, LINE),
        P("net", None, None, None, LINE),
        P("net", None, None, None, LINE),
        P("net", None, None, None, LINE),
    )
    out_specs = (P("net", None, LINE), P("net", None, None, LINE))
    return jax.shard_map(
        on_device, mesh=finer, in_specs=in_specs, out_specs=out_specs, check_vma=False
    )
```

```python
import functools

import jax
import jax.numpy as jnp
from jax import lax
from jax.experimental import pallas as pl
from jax.experimental.pallas import tpu as pltpu
from jax.sharding import Mesh
from jax.sharding import PartitionSpec as P

STEPS = 3
PLANE = ("z", "y")
LINE = ("z", "y", "core")
NET_LINE = ("net", "z", "y", "core")
SIDE = 4
SURGE = 2 * STEPS + 2
CHIPS = SIDE * SIDE
CAPACITY = 5
F32 = jnp.float32
BF16 = jnp.bfloat16
VMEM = pl.BlockSpec(memory_space=pltpu.VMEM)
SMEM = pl.BlockSpec(memory_space=pltpu.SMEM)
PARAMS = pltpu.CompilerParams(vmem_limit_bytes=16 * 1024 * 1024)


def shape(*dims, dtype=F32):
    return jax.ShapeDtypeStruct(dims, dtype)


def estimate(arrays, outs, flops):
    moved = sum(a.size * a.dtype.itemsize for a in [*arrays, *jax.tree.leaves(outs)])
    return pl.CostEstimate(flops=flops, bytes_accessed=moved, transcendentals=0)


def call(kernel, scalars, arrays, outs, scratch=(), flops=1_000_000):
    return pl.pallas_call(
        kernel,
        out_shape=outs,
        in_specs=[SMEM] * len(scalars) + [VMEM] * len(arrays),
        out_specs=jax.tree.map(lambda _: VMEM, outs),
        scratch_shapes=list(scratch),
        compiler_params=PARAMS,
        cost_estimate=estimate(arrays, outs, flops),
    )(*scalars, *arrays)


def halves(x):
    high = x.astype(BF16)
    low = (x - high.astype(F32)).astype(BF16)
    return high, low


def stacked(x):
    return jnp.concatenate(halves(x), axis=0)


def ones_where(mask):
    return jnp.where(mask, 1.0, 0.0).astype(BF16)


def within_block(nodes, block):
    return jnp.clip(nodes - block * 128, -1, 128).astype(F32).astype(BF16)


def hot_block(local, nodes, block):
    one, zero = jnp.ones((), BF16), jnp.zeros((), BF16)
    return jnp.where(local == within_block(nodes, block), one, zero)


def block_places(width):
    return lax.broadcasted_iota(jnp.int32, (128, width), 0).astype(F32).astype(BF16)


def dot(a, b, dims):
    return lax.dot_general(a, b, (dims, ((), ())), preferred_element_type=F32)


def own_core():
    return lax.axis_index("core")


def own_chip():
    return lax.axis_index("z") * SIDE + lax.axis_index("y")


NN = ((1,), (0,))
NT = ((1,), (1,))
TN = ((0,), (0,))


def mix(coef, waves):
    return [
        coef[p, 0:1, :] * waves[0] + coef[p, 1:2, :] * waves[1] + coef[p, 2:3, :] * waves[2]
        for p in range(3)
    ]


def lag_coefficients(own, delay, surge, pw, rw, pa, ra, coef):
    live = own[...]
    steps = delay[...]
    coef[SURGE, 0, 0:1] = surge[...] * live
    coef[SURGE, 0, 1:2] = 2.0 * surge[...] * live
    coef[SURGE, 0, 2:3] = live
    for p in (1, 2):
        coef[SURGE, p] = jnp.zeros(coef.shape[2:], F32)
    first = (steps == 1).astype(F32)
    second = (steps == 2).astype(F32)
    for p in range(3):
        lags = []
        for pole, res in ((pa, ra), (pw, rw)):
            terms = [res[q, p] for q in range(pole.shape[0])]
            for m in range(STEPS):
                if m:
                    terms = [x * pole[q : q + 1, :] for q, x in enumerate(terms)]
                lags.append(sum(terms[1:], terms[0]) * live)
        for m in range(STEPS):
            coef[m, p] = lags[m]
            coef[STEPS + 2 + m, p] = lags[STEPS + m]
        coef[STEPS, p] = lags[STEPS] * first
        coef[STEPS + 1, p] = lags[STEPS + 1] * first + lags[STEPS] * second


def fold_states(times, own, delay, pw, pa, coef, xw, xa, hist, outs):
    live = own[...]
    steps = delay[...]
    delayed = []
    for age in range(max(times) + 1):
        rows = []
        for r in range(3):
            w = None
            for k in range(hist.shape[0] - age):
                part = jnp.where(steps == k + 1 + age, hist[k, r], 0.0)
                w = part if w is None else w + part
            rows.append(w)
        delayed.append(rows)
    for p in range(3):
        totals = {}
        for q in range(pw.shape[0]):
            w_now = xw[q, p]
            a_now = xa[q, p]
            for t in range(max(times) + 1):
                w_now = w_now * pw[q : q + 1, :]
                a_now = a_now * pa[q : q + 1, :]
                if t in times:
                    part = w_now - a_now
                    totals[t] = totals[t] + part if t in totals else part
        for t, out in zip(times, outs):
            value = totals[t] * live
            for s in range(t + 1):
                lag = STEPS + 2 + t - s
                for r in range(3):
                    value = value + coef[lag, p, r : r + 1, :] * delayed[s][r]
            out[p] = value


def fold_first(own, delay, surge, pw, rw, pa, ra, xw, xa, hist, out, coef):
    @pl.when(pl.program_id(0) == 0)
    def _():
        lag_coefficients(own, delay, surge, pw, rw, pa, ra, coef)

    fold_states((0,), own, delay, pw, pa, coef, xw, xa, hist, (out,))


def fold_later(own, delay, pw, pa, coef, xw, xa, hist, *outs):
    fold_states((1, 2), own, delay, pw, pa, coef, xw, xa, hist, outs)


def fold(kernel, small, states, bases, coefs):
    poles, _, scenarios, slots = states[0].shape
    tile = 16
    whole = lambda a: pl.BlockSpec(a.shape, lambda i: (0,) * len(a.shape))
    cut = lambda a: pl.BlockSpec((*a.shape[:2], tile, slots), lambda i: (0, 0, i, 0))
    out = shape(3, scenarios, slots)
    outs = [out] * bases + coefs
    return pl.pallas_call(
        kernel,
        grid=(scenarios // tile,),
        out_shape=outs,
        in_specs=[whole(a) for a in small] + [cut(a) for a in states],
        out_specs=[pl.BlockSpec((3, tile, slots), lambda i: (0, i, 0))] * bases
        + [whole(a) for a in coefs],
        compiler_params=PARAMS,
        cost_estimate=estimate((*small, *states), outs, 20_000_000),
    )(*small, *states)


def split_kernel(inverse, far, mine, other):
    rows = inverse.shape[0]
    for k in range(CHIPS):
        lanes = slice(k * 128, (k + 1) * 128)
        start = pl.multiple_of((k * 2 + own_core()) * 128, 128)
        for block, out in ((inverse, mine), (far, other)):
            high, low = halves(block[:, pl.ds(start, 128)])
            out[0:rows, lanes] = high
            out[rows : 2 * rows, lanes] = low


def gather_into(side, terminal, volts, split, emit):
    count, scenarios, lanes = volts.shape
    for k in range(count):
        high, low = halves(volts[k])
        split[0:scenarios, k * lanes : (k + 1) * lanes] = high
        split[scenarios : 2 * scenarios, k * lanes : (k + 1) * lanes] = low
    width = 256
    local = block_places(width)
    for p in range(3):
        for n in range(terminal.shape[1] // width):
            cut = slice(n * width, (n + 1) * width)
            nodes = terminal[p : p + 1, cut]
            hot = jnp.concatenate(
                [hot_block(local, nodes, 2 * k + side) for k in range(count)], axis=0
            )
            both = dot(split[...], hot, NN)
            emit(p, cut, both[:scenarios] + both[scenarios:])


def gather_kernel(terminal, volts, out, split):
    def emit(p, cut, value):
        out[p, :, cut] = value

    gather_into(own_core(), terminal, volts, split, emit)


def gather_rest(terminal, volts, before, out, split):
    def emit(p, cut, value):
        out[p, :, cut] = before[p, :, cut] + value

    gather_into(1 - own_core(), terminal, volts, split, emit)


def scatter_into(side, terminal, split, emit):
    ends = split.shape[1]
    scenarios = split.shape[0] // 2
    local = block_places(ends)
    nodes = jnp.concatenate([terminal[p : p + 1, :] for p in range(3)], axis=1)
    for k in range(0, CHIPS, 2):
        hot = jnp.concatenate(
            [hot_block(local, nodes, 2 * (k + i) + side) for i in range(2)], axis=0
        )
        both = dot(split, hot, NT)
        value = both[:scenarios] + both[scenarios:]
        for i in range(2):
            emit(k + i, value[:, i * 128 : (i + 1) * 128])


def split_ends(h):
    parts = [stacked(h[p]) for p in range(3)]
    return jnp.concatenate(parts, axis=1)


def scatter_other(terminal, h, ends, out):
    def emit(k, value):
        out[k] = value

    ends[...] = split_ends(h)
    scatter_into(1 - own_core(), terminal, ends[...], emit)


def first_kernel(terminal, volts, before, base, coef, term, h_out, ends, out, split):
    gather_rest(terminal, volts, before, term, split)
    drop = mix(coef[0], term)
    for p in range(3):
        h_out[p] = base[p] - drop[p]
    scatter_other(terminal, h_out, ends, out)


def scatter_mine(step, terminal, ends, source, drain, volts, out):
    def emit(k, value):
        out[k] = value

    scatter_into(own_core(), terminal, ends[...], emit)
    me = own_chip()
    out[me] = out[me] + source[step] - drain[...] * volts[...]


def hot_places(places, count):
    owner = lax.broadcasted_iota(jnp.int32, (count, places.shape[1]), 0)
    return [ones_where(owner * 8 + r == places) for r in range(CAPACITY)]


def packed_lines(values):
    return -(-CAPACITY * values // 128)


def pack_kernel(terminal, volts, before, coef, h, base, *refs):
    *past, term, packed, known, split = refs
    gather_rest(terminal, volts, before, term, split)
    surge2 = coef[SURGE, 0, 1:2, :]
    waves = [surge2 * term[p] - h[p] for p in range(3)]
    high, low = halves(jnp.concatenate(waves, axis=0))
    if len(past) == 1:
        drops = [mix(coef[1], past[0]), mix(coef[0], term)]
        gains = []
    else:
        drops = [mix(coef[2], past[0]), mix(coef[1], past[1]), mix(coef[0], term)]
        gains = [mix(coef[STEPS + 1], past[2])]
    for p in range(3):
        value = base[p]
        for drop in drops:
            value = value - drop[p]
        for gain in gains:
            value = value + gain[p]
        known[p] = value
    lines = packed_lines(high.shape[0])
    owners = packed.shape[0] // lines
    rows = []
    for hot in hot_places(terminal[3:4, :], owners):
        rows.append(dot(hot, high, NT) + dot(hot, low, NT))
    used = sum(r.shape[1] for r in rows)
    rows.append(jnp.zeros((owners, lines * 128 - used), F32))
    rows = jnp.concatenate(rows, axis=1)
    for k in range(lines):
        packed[pl.ds(k, owners, stride=lines), :] = rows[:, k * 128 : (k + 1) * 128]


def arrive_kernel(terminal, packed, base, coef, arrived, h_out, ends, out):
    scenarios = base.shape[1]
    wide = 3 * scenarios
    lines = packed_lines(wide)
    owners = packed.shape[0] // lines
    rows = jnp.concatenate(
        [packed[pl.ds(k, owners, stride=lines), :] for k in range(lines)], axis=1
    )
    total = None
    for r, hot in enumerate(hot_places(terminal[3:4, :], owners)):
        high, low = halves(rows[:, r * wide : (r + 1) * wide])
        part = dot(high, hot, TN) + dot(low, hot, TN)
        total = part if total is None else total + part
    for p in range(3):
        arrived[p] = total[p * scenarios : (p + 1) * scenarios]
    gain = mix(coef[STEPS], arrived)
    for p in range(3):
        h_out[p] = base[p] + gain[p]
    scatter_other(terminal, h_out, ends, out)


def last_kernel(terminal, volts, before, coef, h, out, split):
    surge = coef[SURGE, 0, 0:1, :]

    def emit(p, cut, value):
        term = before[p, :, cut] + value
        out[p, :, cut] = surge[:, cut] * term - h[p, :, cut]

    gather_into(1 - own_core(), terminal, volts, split, emit)


def total_kernel(parts, out):
    total = parts[0]
    for k in range(1, CHIPS):
        total = total + parts[k]
    for k in range(CHIPS):
        out[k] = total


def copies_kernel(a, b, rows, out):
    volts = a[...] + b[...]
    rows[...] = volts
    for k in range(CHIPS):
        out[k] = volts


def solve_kernel(current, inverse, out, split):
    count, scenarios, lanes = current.shape
    for k in range(count):
        high, low = halves(current[k])
        split[0:scenarios, k * lanes : (k + 1) * lanes] = high
        split[scenarios : 2 * scenarios, k * lanes : (k + 1) * lanes] = low
    both = dot(split[...], inverse[...], NT)
    out[...] = both[:scenarios, :lanes] + both[:scenarios, lanes:] + both[scenarios:, :lanes]


def exchanged(x):
    return lax.all_to_all(x, PLANE, 0, 0, tiled=True)


def swapped(x):
    return lax.ppermute(x, "core", [(0, 1), (1, 0)])


def on_device(
    conductance_inverse,
    prior_voltage,
    sources,
    fault_node,
    fault_conductance,
    terminal_node,
    ownership,
    partner,
    delay_steps,
    surge_conductance,
    pole_wave,
    residue_wave,
    pole_admit,
    residue_admit,
    wave_state,
    admit_state,
    wave_history,
):
    rows, node_count = conductance_inverse.shape[1:]
    scenarios = prior_voltage.shape[1]
    slots = ownership.shape[1]
    ends = 3 * slots
    devices = lax.axis_size(NET_LINE)
    net, z, y, core = (lax.axis_index(a) for a in NET_LINE)
    me = lax.axis_index(LINE)

    live = ownership[0] > 0
    live_float = live.astype(F32)[None]
    partners = partner[0]
    slot = jnp.arange(slots, dtype=jnp.int32)
    earlier = (
        (partners[:, None] == partners[None, :])
        & live[:, None]
        & (slot[:, None] < slot[None, :])
    )
    rank = jnp.sum(earlier.astype(jnp.int32), axis=0)
    places = jnp.where(live, partners * 8 + rank, -1)[None]
    table = jnp.concatenate([terminal_node[0], places], axis=0)
    lane = jnp.arange(rows, dtype=jnp.int32)[None]
    first_node = net * node_count + me * rows
    drain = jnp.where(
        fault_node[:, None] - first_node == lane, fault_conductance[:, None], 0.0
    )

    half = shape(CHIPS, scenarios, rows)
    waves = shape(3, scenarios, slots)
    splits = pltpu.VMEM((2 * scenarios, 16 * rows), BF16)
    end_split = shape(2 * scenarios, ends, dtype=BF16)

    block = shape(scenarios, rows)

    def first_gather(plane):
        return call(gather_kernel, (), (table, plane), waves, [splits], 4_000_000_000)

    def finish_constants(states, coef, inverse):
        later = fold(fold_later, (*small, coef), states, STEPS - 1, [])
        share = shape(2 * rows, CHIPS * 128, dtype=BF16)
        mine, other = call(split_kernel, (), inverse, (share, share))
        return later, mine, other

    def reduce(ends_split, other, step, voltage_rows):
        sent = swapped(other)
        mine = call(
            functools.partial(scatter_mine, step),
            (),
            (table, ends_split, sources, drain, voltage_rows),
            half,
            (),
            4_000_000_000,
        )
        return mine + sent

    def solve(currents, inverse_mine, inverse_other):
        plane = exchanged(call(total_kernel, (), (currents,), half))
        other = call(solve_kernel, (), (plane, inverse_other), block, [splits], 500_000_000)
        sent = swapped(other)
        mine = call(solve_kernel, (), (plane, inverse_mine), block, [splits], 500_000_000)
        return call(copies_kernel, (), (mine, sent), (block, half))

    inverse_rows = (conductance_inverse[0], swapped(conductance_inverse[0]))
    voltage_rows = prior_voltage[0]
    plane = exchanged(jnp.broadcast_to(voltage_rows[None], half.shape))
    small = (live_float, delay_steps, pole_wave[0], pole_admit[0])
    states = (wave_state[0], admit_state[0], wave_history[0])
    live_row, delays, poles_w, poles_a = small
    base_0, coef = fold(
        fold_first,
        (
            live_row,
            delays,
            surge_conductance,
            poles_w,
            residue_wave[0],
            poles_a,
            residue_admit[0],
        ),
        states,
        1,
        [shape(SURGE + 1, 3, 3, slots)],
    )
    plane, base_0, coef, table = lax.optimization_barrier((plane, base_0, coef, table))
    far = swapped(plane)
    before = first_gather(plane)
    t0, h, ends_split, other = call(
        first_kernel,
        (),
        (table, far, before, base_0, coef),
        (waves, waves, end_split, half),
        [splits],
        8_000_000_000,
    )
    currents, *inputs = lax.optimization_barrier(
        (reduce(ends_split, other, 0, voltage_rows), states, coef, inverse_rows)
    )
    constants = finish_constants(*inputs)
    currents = exchanged(currents)
    currents, constants = lax.optimization_barrier((currents, constants))
    later, *inverses = constants
    base = [base_0, *later]
    voltage_rows, copies = solve(currents, *inverses)
    terms = [t0]
    arrivals = []
    lines = packed_lines(3 * scenarios)
    packed_shape = shape(devices * lines, 128)
    for step in range(1, STEPS):
        plane = exchanged(copies)
        far = swapped(plane)
        before = first_gather(plane)
        term, packed, known = call(
            pack_kernel,
            (),
            (table, far, before, coef, h, base[step], *terms, *arrivals),
            (waves, packed_shape, waves),
            [splits],
            5_000_000_000,
        )
        terms.append(term)
        packed = packed.reshape(devices, 1, lines * 128)
        packed = lax.all_to_all(packed, NET_LINE, 0, 0, tiled=True)
        packed = packed.reshape(devices * lines, 128)
        arrived, h, ends_split, other = call(
            arrive_kernel,
            (),
            (table, packed, known, coef),
            (waves, waves, end_split, half),
            (),
            5_000_000_000,
        )
        arrivals.append(arrived)
        currents = exchanged(reduce(ends_split, other, step, voltage_rows))
        voltage_rows, copies = solve(currents, *inverses)
    plane = exchanged(copies)
    far = swapped(plane)
    before = first_gather(plane)
    current = call(
        last_kernel, (), (table, far, before, coef, h), waves, [splits], 4_000_000_000
    )
    return voltage_rows[None], current[None]


def solution(mesh):
    finer = Mesh(mesh.devices.reshape(mesh.shape["net"], SIDE, SIDE, 2), NET_LINE)
    in_specs = (
        P("net", LINE, None),
        P("net", None, LINE),
        P(None, "net", LINE),
        P(),
        P(),
        P("net", None, LINE),
        P("net", LINE),
        P("net", LINE),
        P("net", LINE),
        P("net", LINE),
        P("net", None, LINE),
        P("net", None, None, None, LINE),
        P("net", None, LINE),
        P("net", None, None, None, LINE),
        P("net", None, None, None, LINE),
        P("net", None, None, None, LINE),
        P("net", None, None, None, LINE),
    )
    out_specs = (P("net", None, LINE), P("net", None, None, LINE))
    return jax.shard_map(
        on_device, mesh=finer, in_specs=in_specs, out_specs=out_specs, check_vma=False
    )
```
